32 devices in a mesh: rep: 8 (over z, x), fsdp: 4 (over y, core).
Axes of the slice: x: 2, y: 2, z: 4, core: 2. Of those that a mesh axis runs over, the one named last changes fastest.
Arguments:
- tokens: bfloat16 [6144, 4096], P(('rep', 'fsdp')), may hold values from -6 to 6
- quant_weight: bfloat16 [4096, 512], P('fsdp'), may hold values from -6 to 6
- block_scales: bfloat16 [1024], P('fsdp'), may hold values from 0.0069885254 to 0.031982422
- key_grad: bfloat16 [6144, 512], P(('rep', 'fsdp')), may hold values from -6 to 6
Outputs:
- rotated: bfloat16 [6144, 512], P(('rep', 'fsdp'))
- token_grad: bfloat16 [6144, 4096], P(('rep', 'fsdp'))
- weight_grad: bfloat16 [4096, 512], P(('rep', 'fsdp'))
The draws below stay inside these ranges and needn't reach their ends.
All inputs are finite; a program needn't handle non-finite values.
Results may differ from the reference program's by a relative error of at most 0.023.
Values may be sent and summed in bfloat16 or wider, within the bound.
A program may use at most 64 MiB of HBM per device.

```python
import math
import jax
import jax.numpy as jnp
from jax import lax

DW = 4096
HEAD_DIM = 128
QBLOCK = 2048
TOK_DEV = 192
KVW = 512
TOKENS = 6144
N_REP = 8
N_FSDP = 4


def strengthened(result, rng, source, target, parts, factor):
    owner, partner = [(jnp.arange(result.shape[position]) // (result.shape[position] // parts)).reshape([-1 if axis == position else 1 for axis in range(result.ndim)]) for position in (source, target)]
    chosen = jax.random.permutation(rng, parts)[partner]
    strong = (owner == chosen) | (owner == (partner + parts // 2) % parts)
    return jnp.where(strong, factor * result, result)


def block_scale(key, shape, shards, low, high):
    def one(dim, parts):
        heights = jax.random.uniform(jax.random.fold_in(jax.random.fold_in(key, 6), dim), (parts,), jnp.float32, low / len(shards), high / len(shards))
        return jnp.repeat(jnp.exp(heights), shape[dim] // parts).reshape((-1,) + (1,) * (len(shape) - dim - 1))

    loudness = one(*shards[0])
    for cut in shards[1:]:
        loudness = loudness * one(*cut)
    return loudness


def bell_draw(key, extent, width, reach, shards=(), kind=jnp.bfloat16):
    result = jax.random.normal(key, extent, jnp.float32) * width
    if len(shards) > 0:
        result = block_scale(key, extent, shards, -0.22, 0.18) * result
    return jnp.clip(result, min=-reach, max=reach).astype(kind)


def noise_with(key, shape, spread, reach, split, heavy, held_as=jnp.bfloat16):
    result = spread * jax.random.normal(key, shape, jnp.float32)
    if split:
        result = result * block_scale(key, shape, split, -0.22, 0.18)
    return jnp.clip(strengthened(result, jax.random.fold_in(key, 3), *heavy), -reach, reach).astype(held_as)


def setup_inputs(seed: int = 0) -> dict:
    seeds = jax.random.split(jax.random.key(seed), 5)
    tokens = noise_with(seeds[0], (TOKENS, DW), 1.0, 6.0, ((0, 32),), (0, 1, 32, 2.75))
    quant_weight = bell_draw(seeds[1], (DW, KVW), 1.0, 6.0, ((0, 4),))
    block_scales = jnp.clip(jnp.exp(math.log(0.031982422) - 1.52091686 * jax.random.uniform(seeds[2], (DW * KVW // QBLOCK,), jnp.float32) ** block_scale(seeds[2], (DW * KVW // QBLOCK,), ((0, 4),), -0.2, 0.2)), 0.0069885254, 0.031982422).astype(jnp.bfloat16)
    key_grad = bell_draw(seeds[3], (TOKENS, KVW), 1.0, 6.0, ((0, 32),))
    return {"tokens": tokens, "quant_weight": quant_weight, "block_scales": block_scales, "key_grad": key_grad}


rope_base = 10000.0

def dequantize(quant_weight, block_scales):
    rows_per_block = quant_weight.shape[0] // block_scales.shape[0]
    scaled = quant_weight.astype(jnp.float32).reshape(block_scales.shape[0], rows_per_block, quant_weight.shape[1])
    scaled = scaled * block_scales.astype(jnp.float32)[:, None, None]
    return scaled.reshape(quant_weight.shape).astype(jnp.bfloat16)

def rotary(projected, positions, direction):
    half_size = HEAD_DIM // 2
    steps = jnp.arange(half_size, dtype=jnp.int32).astype(jnp.float32)
    frequency = jnp.exp(steps * (-2.0 * math.log(rope_base) / HEAD_DIM))
    angles = positions[:, None] * frequency[None, :]
    cosine = jnp.cos(angles)[:, None, :]
    sine_part = direction * jnp.sin(angles)[:, None, :]
    halves = projected.reshape(projected.shape[0], -1, 2, half_size)
    leading = halves[:, :, 0]
    trailing = halves[:, :, 1]
    turned = jnp.stack([leading * cosine - trailing * sine_part, trailing * cosine + leading * sine_part], axis=2)
    return turned.reshape(projected.shape)

def reference(tokens, quant_weight, block_scales, key_grad):
    weight = dequantize(quant_weight, block_scales)
    device_count = N_REP * N_FSDP
    token_blocks = tokens.reshape(device_count, TOK_DEV, DW)
    grad_blocks = key_grad.reshape(device_count, TOK_DEV, KVW)
    offsets = jnp.arange(TOK_DEV, dtype=jnp.int32)

    def scan_step(running, inputs):
        token_block, key_block, device_index = inputs
        positions = (device_index % N_FSDP * TOK_DEV + offsets).astype(jnp.float32)
        projected = jnp.dot(token_block, weight, preferred_element_type=jnp.float32)
        rotated = rotary(projected, positions, 1.0).astype(jnp.bfloat16)
        proj_grad = rotary(key_block.astype(jnp.float32), positions, -1.0).astype(jnp.bfloat16)
        token_grad = jnp.dot(proj_grad, weight.T, preferred_element_type=jnp.float32).astype(jnp.bfloat16)
        partial_value = jnp.dot(token_block.T, proj_grad, preferred_element_type=jnp.float32).astype(jnp.bfloat16)
        partial_value = lax.optimization_barrier(partial_value)
        return (running + partial_value.astype(jnp.float32), (rotated, token_grad))
    start_sum = jnp.zeros((DW, KVW), jnp.float32)
    indices = jnp.arange(device_count, dtype=jnp.int32)
    summed, (rotated, token_grad) = lax.scan(scan_step, start_sum, (token_blocks, grad_blocks, indices))
    weight_grad = (summed * (1.0 / math.sqrt(TOKENS))).astype(jnp.bfloat16)
    return (rotated.reshape(TOKENS, KVW), token_grad.reshape(TOKENS, DW), weight_grad)
```

```python
import math

import jax
import jax.numpy as jnp
from jax import lax
from jax.experimental import pallas as pl
from jax.experimental.pallas import tpu as pltpu
from jax.sharding import PartitionSpec as P

HEAD_DIM = 128


rope_base = 10000.0


def dequantize(quant_weight, block_scales):
    rows_per_block = quant_weight.shape[0] // block_scales.shape[0]
    scaled = quant_weight.astype(jnp.float32).reshape(
        block_scales.shape[0], rows_per_block, quant_weight.shape[1]
    )
    scaled = scaled * block_scales.astype(jnp.float32)[:, None, None]
    return scaled.reshape(quant_weight.shape).astype(jnp.bfloat16)


def rotary(projected, positions, direction):
    half_size = HEAD_DIM // 2
    steps = jnp.arange(half_size, dtype=jnp.int32).astype(jnp.float32)
    frequency = jnp.exp(steps * (-2.0 * math.log(rope_base) / HEAD_DIM))
    angles = positions[:, None] * frequency[None, :]
    cosine = jnp.cos(angles)[:, None, :]
    sine_part = direction * jnp.sin(angles)[:, None, :]
    halves = projected.reshape(projected.shape[0], -1, 2, half_size)
    leading = halves[:, :, 0]
    trailing = halves[:, :, 1]
    turned = jnp.stack(
        [leading * cosine - trailing * sine_part, trailing * cosine + leading * sine_part], axis=2
    )
    return turned.reshape(projected.shape)


def partial_rows(source, proj_grad):
    return lax.dot_general(
        source, proj_grad, (((0,), (0,)), ((), ())), preferred_element_type=jnp.float32
    )


def body(tokens, quant_weight, block_scales, key_grad):
    row_count = tokens.shape[0]
    all_codes, all_scales = (
        lax.all_gather(quant_weight, "fsdp", axis=0, tiled=True),
        lax.all_gather(block_scales, "fsdp", axis=0, tiled=True),
    )
    weight = dequantize(all_codes, all_scales)
    positions = (
        lax.axis_index("fsdp") * row_count + jnp.arange(row_count, dtype=jnp.int32)
    ).astype(jnp.float32)
    projected = jnp.dot(tokens, weight, preferred_element_type=jnp.float32)
    rotated = rotary(projected, positions, 1.0).astype(jnp.bfloat16)
    proj_grad = rotary(key_grad.astype(jnp.float32), positions, -1.0).astype(jnp.bfloat16)
    token_grad = lax.dot_general(
        proj_grad, weight, (((1,), (1,)), ((), ())), preferred_element_type=jnp.float32
    ).astype(jnp.bfloat16)
    total_rows = weight.shape[0]
    fsdp_size = lax.axis_size("fsdp")
    rep_size = lax.axis_size("rep")
    share = total_rows // (fsdp_size * rep_size)
    reordered = (
        tokens.reshape(row_count, rep_size, fsdp_size, share)
        .transpose(0, 2, 1, 3)
        .reshape(row_count, total_rows)
    )
    group_sum = lax.psum_scatter(
        partial_rows(reordered, proj_grad).astype(jnp.bfloat16),
        "fsdp",
        scatter_dimension=0,
        tiled=True,
    ).astype(jnp.float32)
    summed = lax.psum_scatter(group_sum, "rep", scatter_dimension=0, tiled=True)
    weight_grad = (summed * (1.0 / math.sqrt(row_count * fsdp_size * rep_size))).astype(
        jnp.bfloat16
    )
    return (rotated, token_grad, weight_grad)


MESH = pl.DeviceIdType.MESH


def fused_kernel(
    tok_ref, quant_ref, scale_ref, kg_ref,
    rot_ref, tg_ref, wg_ref,
    wbuf, tok_twin, pg, proj, cos_t, sin_t,
    s_a, s_b, s_c, a1, b1, c1, a2, b2, c2, a3, b3, c3, a4, b4, c4,
    tok_sem, pg_sem, w_send, w_recv, rs_send, rs_recv,
):
    rep, fsdp = lax.axis_index("rep"), lax.axis_index("fsdp")
    x, z0, z1 = rep % 2, (rep // 2) % 2, rep // 4
    y, c = fsdp // 2, fsdp % 2
    twin = (rep, fsdp + 1 - 2 * c)
    over_y = (rep, fsdp + 2 - 4 * y)
    over_x = (rep + 1 - 2 * x, fsdp)
    over_z0 = (rep + 2 - 4 * z0, fsdp)
    over_z1 = (rep + 4 - 8 * z1, fsdp)
    row_count, width = kg_ref.shape
    shard_rows = quant_ref.shape[0]
    piece = shard_rows // 4
    block = wg_ref.shape[0]

    barrier = pltpu.get_barrier_semaphore()
    for other in (twin, over_y, over_x, over_z0, over_z1):
        pl.semaphore_signal(barrier, inc=1, device_id=other, device_id_type=MESH)
    pl.semaphore_wait(barrier, 5)

    started = []

    def send(src, dst, send_sem, recv_sem, to):
        copy = pltpu.make_async_remote_copy(
            src_ref=src, dst_ref=dst, send_sem=send_sem, recv_sem=recv_sem,
            device_id=to, device_id_type=MESH,
        )
        copy.start()
        started.append(copy)
        return copy

    def send_tokens(j, carry):
        col = pl.multiple_of((2 * j + 1 - c) * block, block)
        pltpu.make_async_remote_copy(
            src_ref=tok_ref.at[:, pl.ds(col, block)], dst_ref=tok_twin.at[j],
            send_sem=tok_sem.at[0], recv_sem=tok_sem.at[1],
            device_id=twin, device_id_type=MESH,
        ).start()
        return carry

    lax.fori_loop(0, 16, send_tokens, 0)
    all_tokens = pltpu.make_async_remote_copy(
        src_ref=tok_twin, dst_ref=tok_twin, send_sem=tok_sem.at[0], recv_sem=tok_sem.at[1],
        device_id=twin, device_id_type=MESH,
    )

    def dequant(i):
        rows = pl.ds(pl.multiple_of(i * piece, piece), piece)
        n_blocks = scale_ref.shape[1]
        per_block = shard_rows // n_blocks
        owner = (i * piece + lax.broadcasted_iota(jnp.int32, (piece, n_blocks), 0)) // per_block
        lane = lax.broadcasted_iota(jnp.int32, (piece, n_blocks), 1)
        picked = jnp.where(owner == lane, scale_ref[...].astype(jnp.float32), 0.0)
        column = jnp.sum(picked, axis=1, keepdims=True)
        wbuf[fsdp, i] = (quant_ref[rows, :].astype(jnp.float32) * column).astype(jnp.bfloat16)

    def send_w(shard, i, slot, to):
        return send(
            wbuf.at[shard, i], wbuf.at[shard, i], w_send.at[slot], w_recv.at[slot], to
        )

    from_y = []
    for q in range(2):
        dequant(2 * x + q)
        from_y.append(send_w(fsdp, 2 * x + q, q, over_y))

    shape = (row_count, HEAD_DIM)
    half = HEAD_DIM // 2
    lane = lax.broadcasted_iota(jnp.int32, shape, 1)
    steps = (lane % half).astype(jnp.float32)
    frequency = jnp.exp(steps * (-2.0 * math.log(rope_base) / HEAD_DIM))
    place = (fsdp * row_count + lax.broadcasted_iota(jnp.int32, shape, 0)).astype(jnp.float32)
    angles = place * frequency
    cos_t[...] = jnp.cos(angles)
    sine = jnp.sin(angles)
    sin_t[...] = jnp.where(lane < half, -sine, sine)

    def turn(value, direction):
        return value * cos_t[...] + pltpu.roll(value, half, 1) * (direction * sin_t[...])

    heads = width // HEAD_DIM
    for h in range(heads):
        cols = slice(h * HEAD_DIM, (h + 1) * HEAD_DIM)
        pg[0, :, cols] = turn(kg_ref[:, cols].astype(jnp.float32), -1.0).astype(jnp.bfloat16)
    pg_copy = send(pg.at[0], pg.at[1], pg_sem.at[0], pg_sem.at[1], twin)

    for q in range(2):
        dequant(2 * (1 - x) + q)
    own_half = [
        send(
            wbuf.at[fsdp, pl.ds(2 * h, 2)], wbuf.at[fsdp, pl.ds(2 * h, 2)],
            w_send.at[2 + h], w_recv.at[2 + h], twin,
        )
        for h in range(2)
    ]

    all_tokens.wait_recv()
    pg_copy.wait_recv()

    def blocks(bx, by, bz0):
        def one(bz1, carry):
            index = bz1 * 8 + bz0 * 4 + bx * 2 + by
            col = pl.multiple_of((2 * index + c) * block, block)
            left = jnp.concatenate([tok_ref[:, pl.ds(col, block)], tok_twin[index]], axis=0)
            right = pg[...].reshape(2 * row_count, width)
            total = lax.dot_general(
                left, right, (((0,), (0,)), ((), ())), preferred_element_type=jnp.float32
            ).astype(jnp.bfloat16)
            quarter = block // 4
            s_a[bx, by, bz0, bz1] = total[:quarter]
            s_b[by, bz0, bx, bz1] = total[quarter : 2 * quarter]
            s_c[bz0, bx, by, bz1] = total[2 * quarter :]
            return carry

        lax.fori_loop(0, 2, one, 0)

    class Flow:
        def __init__(self, index, bits, others, bufs):
            self.index, self.bits, self.others, self.bufs = index, bits, others, bufs
            self.copies = {}

        def launch(self, stage, part):
            bits, bufs = self.bits, self.bufs
            slot = self.index * 8 + stage * 2 + part
            sems = (rs_send.at[slot], rs_recv.at[slot], self.others[stage])
            lead = 1 - bits[stage]
            if stage == 3:
                src, dst = bufs[3].at[lead], bufs[4]
            else:
                sub = 1 - bits[stage + 1] if part == 0 else bits[stage + 1]
                src, dst = bufs[stage].at[lead, sub], bufs[stage + 1].at[sub]
            self.copies[stage, part] = send(src, dst, *sems)

        def take(self, stage, part):
            bits, bufs = self.bits, self.bufs
            self.copies[stage, part].wait_recv()
            sub = 1 - bits[stage + 1] if part == 0 else bits[stage + 1]
            mine = bufs[stage][bits[stage], sub].astype(jnp.float32)
            bufs[stage + 1][sub] = (
                bufs[stage + 1][sub].astype(jnp.float32) + mine
            ).astype(jnp.bfloat16)
            if part == 0:
                self.launch(stage + 1, 0)
                if stage + 1 < 3:
                    self.launch(stage + 1, 1)

        def finish(self, rows):
            bits, bufs = self.bits, self.bufs
            self.copies[3, 0].wait_recv()
            total = bufs[4][...].astype(jnp.float32) + bufs[3][bits[3]].astype(jnp.float32)
            count = row_count * lax.axis_size("rep") * lax.axis_size("fsdp")
            wg_ref[rows, :] = (total * (1.0 / math.sqrt(count))).astype(jnp.bfloat16)

    fa = Flow(0, (x, y, z0, z1), (over_x, over_y, over_z0, over_z1), (s_a, a1, a2, a3, a4))
    fb = Flow(1, (y, z0, x, z1), (over_y, over_z0, over_x, over_z1), (s_b, b1, b2, b3, b4))
    fc = Flow(2, (z0, x, y, z1), (over_z0, over_x, over_y, over_z1), (s_c, c1, c2, c3, c4))

    blocks(1 - x, 1 - y, 1 - z0)
    blocks(1 - x, y, 1 - z0)
    fc.launch(0, 0)
    blocks(1 - x, 1 - y, z0)
    fa.launch(0, 0)
    blocks(x, 1 - y, 1 - z0)
    fb.launch(0, 0)
    blocks(x, y, 1 - z0)
    fc.launch(0, 1)
    blocks(1 - x, y, z0)
    fa.launch(0, 1)
    blocks(x, 1 - y, z0)
    fb.launch(0, 1)
    blocks(x, y, z0)

    proj[...] = jnp.zeros_like(proj)

    def use(shard, first, count):
        def one(i, carry):
            at = first + i
            col = pl.multiple_of(shard * shard_rows + at * piece, piece)
            w = wbuf[shard, at]
            tg_ref[:, pl.ds(col, piece)] = lax.dot_general(
                pg[0], w, (((1,), (1,)), ((), ())), preferred_element_type=jnp.float32
            ).astype(jnp.bfloat16)
            proj[...] += jnp.dot(
                tok_ref[:, pl.ds(col, piece)], w, preferred_element_type=jnp.float32
            )
            return carry

        lax.fori_loop(0, count, one, 0)

    side = fsdp + 2 - 4 * y
    twin_shard = fsdp + 1 - 2 * c
    twin_side = side + 1 - 2 * c

    from_x, from_twin = [], []

    def forward(q):
        from_y[q].wait_recv()
        from_x.append(send_w(side, 2 * x + q, 4 + q, over_x))
        from_twin.append(send_w(side, 2 * x + q, 6 + q, twin))

    def forward_x(q):
        from_x[q].wait_recv()
        from_twin.append(send_w(side, 2 * (1 - x) + q, 8 + q, twin))

    use(fsdp, 0, 4)
    forward(0)
    for copy in own_half:
        copy.wait_recv()
    use(twin_shard, 0, 4)
    fa.take(0, 0)
    fa.take(0, 1)
    forward(1)
    fc.take(0, 0)
    fb.take(0, 0)
    forward_x(0)
    fc.take(0, 1)
    fa.take(1, 0)
    fb.take(0, 1)
    use(side, 2 * x, 2)
    fa.take(1, 1)
    fb.take(1, 0)
    fc.take(1, 0)
    fa.take(2, 0)
    fb.take(1, 1)
    fc.take(1, 1)
    fa.take(2, 1)
    fb.take(2, 0)
    fc.take(2, 0)
    fb.take(2, 1)
    fc.take(2, 1)
    forward_x(1)
    from_twin[0].wait_recv()
    from_twin[1].wait_recv()
    use(twin_side, 2 * x, 2)
    use(side, 2 * (1 - x), 2)
    quarter = block // 4
    fa.finish(slice(0, quarter))
    fb.finish(slice(quarter, 2 * quarter))
    fc.finish(slice(2 * quarter, block))
    from_twin[2].wait_recv()
    from_twin[3].wait_recv()
    use(twin_side, 2 * (1 - x), 2)
    for h in range(heads):
        cols = slice(h * HEAD_DIM, (h + 1) * HEAD_DIM)
        rot_ref[:, cols] = turn(proj[:, cols], 1.0).astype(jnp.bfloat16)

    all_tokens.wait_send()
    for copy in started:
        copy.wait_send()


def fused_body(tokens, quant_weight, block_scales, key_grad):
    row_count, model = tokens.shape
    shard_rows, width = quant_weight.shape
    block = model // (lax.axis_size("rep") * lax.axis_size("fsdp"))
    quarter = block // 4
    bf16, f32 = jnp.bfloat16, jnp.float32
    vmem = pl.BlockSpec(memory_space=pltpu.VMEM)
    tall = (quarter, quarter, 2 * quarter)
    flows = [
        pltpu.VMEM((2,) * (4 - level) + (rows, width), bf16)
        for level in range(5)
        for rows in tall
    ]
    return pl.pallas_call(
        fused_kernel,
        out_shape=[
            jax.ShapeDtypeStruct((row_count, width), bf16),
            jax.ShapeDtypeStruct((row_count, model), bf16),
            jax.ShapeDtypeStruct((block, width), bf16),
        ],
        in_specs=[vmem] * 4,
        out_specs=[vmem] * 3,
        scratch_shapes=[
            pltpu.VMEM((4, 4, shard_rows // 4, width), bf16),
            pltpu.VMEM((16, row_count, block), bf16),
            pltpu.VMEM((2, row_count, width), bf16),
            pltpu.VMEM((row_count, width), f32),
            pltpu.VMEM((row_count, HEAD_DIM), f32),
            pltpu.VMEM((row_count, HEAD_DIM), f32),
            *flows,
            pltpu.SemaphoreType.DMA((2,)),
            pltpu.SemaphoreType.DMA((2,)),
            pltpu.SemaphoreType.DMA((10,)),
            pltpu.SemaphoreType.DMA((10,)),
            pltpu.SemaphoreType.DMA((24,)),
            pltpu.SemaphoreType.DMA((24,)),
        ],
        compiler_params=pltpu.CompilerParams(
            collective_id=0, has_side_effects=True, vmem_limit_bytes=40 * 1024 * 1024
        ),
    )(tokens, quant_weight, block_scales.reshape(1, -1), key_grad)


def solution(mesh):
    paired = mesh.shape["rep"] == 8 and mesh.shape["fsdp"] == 4
    return jax.shard_map(
        fused_body if paired else body,
        mesh=mesh,
        in_specs=(P(("rep", "fsdp"), None), P("fsdp", None), P("fsdp"), P(("rep", "fsdp"), None)),
        out_specs=(P(("rep", "fsdp"), None), P(("rep", "fsdp"), None), P(("rep", "fsdp"), None)),
        check_vma=False,
    )
```

```python
import math

import jax
import jax.numpy as jnp
from jax import lax
from jax.experimental import pallas as pl
from jax.experimental.pallas import tpu as pltpu
from jax.sharding import PartitionSpec as P

HEAD_DIM = 128


rope_base = 10000.0


def dequantize(quant_weight, block_scales):
    rows_per_block = quant_weight.shape[0] // block_scales.shape[0]
    scaled = quant_weight.astype(jnp.float32).reshape(
        block_scales.shape[0], rows_per_block, quant_weight.shape[1]
    )
    scaled = scaled * block_scales.astype(jnp.float32)[:, None, None]
    return scaled.reshape(quant_weight.shape).astype(jnp.bfloat16)


def rotary(projected, positions, direction):
    half_size = HEAD_DIM // 2
    steps = jnp.arange(half_size, dtype=jnp.int32).astype(jnp.float32)
    frequency = jnp.exp(steps * (-2.0 * math.log(rope_base) / HEAD_DIM))
    angles = positions[:, None] * frequency[None, :]
    cosine = jnp.cos(angles)[:, None, :]
    sine_part = direction * jnp.sin(angles)[:, None, :]
    halves = projected.reshape(projected.shape[0], -1, 2, half_size)
    leading = halves[:, :, 0]
    trailing = halves[:, :, 1]
    turned = jnp.stack(
        [leading * cosine - trailing * sine_part, trailing * cosine + leading * sine_part], axis=2
    )
    return turned.reshape(projected.shape)


def partial_rows(source, proj_grad):
    return lax.dot_general(
        source, proj_grad, (((0,), (0,)), ((), ())), preferred_element_type=jnp.float32
    )


def body(tokens, quant_weight, block_scales, key_grad):
    row_count = tokens.shape[0]
    all_codes, all_scales = (
        lax.all_gather(quant_weight, "fsdp", axis=0, tiled=True),
        lax.all_gather(block_scales, "fsdp", axis=0, tiled=True),
    )
    weight = dequantize(all_codes, all_scales)
    positions = (
        lax.axis_index("fsdp") * row_count + jnp.arange(row_count, dtype=jnp.int32)
    ).astype(jnp.float32)
    projected = jnp.dot(tokens, weight, preferred_element_type=jnp.float32)
    rotated = rotary(projected, positions, 1.0).astype(jnp.bfloat16)
    proj_grad = rotary(key_grad.astype(jnp.float32), positions, -1.0).astype(jnp.bfloat16)
    token_grad = lax.dot_general(
        proj_grad, weight, (((1,), (1,)), ((), ())), preferred_element_type=jnp.float32
    ).astype(jnp.bfloat16)
    total_rows = weight.shape[0]
    fsdp_size = lax.axis_size("fsdp")
    rep_size = lax.axis_size("rep")
    share = total_rows // (fsdp_size * rep_size)
    reordered = (
        tokens.reshape(row_count, rep_size, fsdp_size, share)
        .transpose(0, 2, 1, 3)
        .reshape(row_count, total_rows)
    )
    group_sum = lax.psum_scatter(
        partial_rows(reordered, proj_grad).astype(jnp.bfloat16),
        "fsdp",
        scatter_dimension=0,
        tiled=True,
    ).astype(jnp.float32)
    summed = lax.psum_scatter(group_sum, "rep", scatter_dimension=0, tiled=True)
    weight_grad = (summed * (1.0 / math.sqrt(row_count * fsdp_size * rep_size))).astype(
        jnp.bfloat16
    )
    return (rotated, token_grad, weight_grad)


MESH = pl.DeviceIdType.MESH


def fused_kernel(
    tok_hbm, quant_hbm, scale_ref, kg_hbm,
    rot_ref, tg_hbm, wg_ref,
    tok_ref, quant_ref, kg_ref, tg_ref,
    wbuf, tok_twin, pg, proj, cos_t, sin_t,
    s_a, s_b, a1, b1, a2, b2, a3, b3, a4, b4,
    load_sem, store_sem, tok_sem, pg_sem, w_send, w_recv, rs_send, rs_recv,
):
    rep, fsdp = lax.axis_index("rep"), lax.axis_index("fsdp")
    x, z0, z1 = rep % 2, (rep // 2) % 2, rep // 4
    y, c = fsdp // 2, fsdp % 2
    twin = (rep, fsdp + 1 - 2 * c)
    over_y = (rep, fsdp + 2 - 4 * y)
    over_x = (rep + 1 - 2 * x, fsdp)
    over_z0 = (rep + 2 - 4 * z0, fsdp)
    over_z1 = (rep + 4 - 8 * z1, fsdp)
    row_count, width = kg_ref.shape
    shard_rows = quant_ref.shape[0]
    piece = shard_rows // 4
    part = shard_rows // 8
    block = wg_ref.shape[0]
    here = 2 * x + z0

    load_quant = pltpu.make_async_copy(quant_hbm, quant_ref, load_sem.at[0])
    load_quant.start()
    load_kg = pltpu.make_async_copy(kg_hbm, kg_ref, load_sem.at[1])
    load_kg.start()
    load_tok = pltpu.make_async_copy(tok_hbm, tok_ref, load_sem.at[2])
    load_tok.start()

    barrier = pltpu.get_barrier_semaphore()
    for other in (twin, over_y, over_x, over_z0, over_z1):
        pl.semaphore_signal(barrier, inc=1, device_id=other, device_id_type=MESH)

    def dequant(i):
        rows = pl.ds(pl.multiple_of(i * part, part), part)
        n_blocks = scale_ref.shape[1]
        per_block = shard_rows // n_blocks
        owner = (i * part + lax.broadcasted_iota(jnp.int32, (part, n_blocks), 0)) // per_block
        lane = lax.broadcasted_iota(jnp.int32, (part, n_blocks), 1)
        picked = jnp.where(owner == lane, scale_ref[...].astype(jnp.float32), 0.0)
        column = jnp.sum(picked, axis=1, keepdims=True)
        wbuf[fsdp, i] = (quant_ref[rows, :].astype(jnp.float32) * column).astype(jnp.bfloat16)

    load_quant.wait()
    dequant(2 * here)
    dequant(2 * here + 1)
    pl.semaphore_wait(barrier, 5)

    started = []

    def send(src, dst, send_sem, recv_sem, to):
        copy = pltpu.make_async_remote_copy(
            src_ref=src, dst_ref=dst, send_sem=send_sem, recv_sem=recv_sem,
            device_id=to, device_id_type=MESH,
        )
        copy.start()
        started.append(copy)
        return copy

    def send_w(shard, i, slot, to):
        return send(
            wbuf.at[shard, i], wbuf.at[shard, i], w_send.at[slot], w_recv.at[slot], to
        )

    from_y = [send_w(fsdp, 2 * here + q, q, over_y) for q in range(2)]

    def send_tokens(j, carry):
        col = pl.multiple_of((2 * j + 1 - c) * block, block)
        pltpu.make_async_remote_copy(
            src_ref=tok_hbm.at[:, pl.ds(col, block)], dst_ref=tok_twin.at[j],
            send_sem=tok_sem.at[0], recv_sem=tok_sem.at[1],
            device_id=twin, device_id_type=MESH,
        ).start()
        return carry

    lax.fori_loop(0, 16, send_tokens, 0)
    all_tokens = pltpu.make_async_remote_copy(
        src_ref=tok_twin, dst_ref=tok_twin, send_sem=tok_sem.at[0], recv_sem=tok_sem.at[1],
        device_id=twin, device_id_type=MESH,
    )

    shape = (row_count, HEAD_DIM)
    half = HEAD_DIM // 2
    lane = lax.broadcasted_iota(jnp.int32, shape, 1)
    steps = (lane % half).astype(jnp.float32)
    frequency = jnp.exp(steps * (-2.0 * math.log(rope_base) / HEAD_DIM))
    place = (fsdp * row_count + lax.broadcasted_iota(jnp.int32, shape, 0)).astype(jnp.float32)
    angles = place * frequency
    cos_t[...] = jnp.cos(angles)
    sine = jnp.sin(angles)
    sin_t[...] = jnp.where(lane < half, -sine, sine)

    def turn(value, direction):
        return value * cos_t[...] + pltpu.roll(value, half, 1) * (direction * sin_t[...])

    heads = width // HEAD_DIM
    load_kg.wait()
    for h in range(heads):
        cols = slice(h * HEAD_DIM, (h + 1) * HEAD_DIM)
        pg[0, :, cols] = turn(kg_ref[:, cols].astype(jnp.float32), -1.0).astype(jnp.bfloat16)
    pg_copy = send(pg.at[0], pg.at[1], pg_sem.at[0], pg_sem.at[1], twin)

    def dequant_other(i, carry):
        other = (2 * here + 2 + i) % 8
        dequant(other)
        return carry

    lax.fori_loop(0, 6, dequant_other, 0)
    load_tok.wait()
    all_tokens.wait_recv()
    pg_copy.wait_recv()
    own = send(wbuf.at[fsdp], wbuf.at[fsdp], w_send.at[16], w_recv.at[16], twin)

    def blocks(bx, by):
        def one(bz, carry):
            bz0, bz1 = bz // 2, bz % 2
            index = bz1 * 8 + bz0 * 4 + bx * 2 + by
            col = pl.multiple_of((2 * index + c) * block, block)
            left = jnp.concatenate([tok_ref[:, pl.ds(col, block)], tok_twin[index]], axis=0)
            right = pg[...].reshape(2 * row_count, width)
            total = lax.dot_general(
                left, right, (((0,), (0,)), ((), ())), preferred_element_type=jnp.float32
            ).astype(jnp.bfloat16)
            s_a[bx, by, bz0, bz1] = total[: block // 2]
            s_b[by, bx, bz0, bz1] = total[block // 2 :]
            return carry

        lax.fori_loop(0, 4, one, 0)

    class Flow:
        def __init__(self, index, bits, others, bufs):
            self.index, self.bits, self.others, self.bufs = index, bits, others, bufs
            self.copies = {}

        def launch(self, stage, turn_of):
            bits, bufs = self.bits, self.bufs
            slot = self.index * 8 + stage * 2 + turn_of
            sems = (rs_send.at[slot], rs_recv.at[slot], self.others[stage])
            lead = 1 - bits[stage]
            if stage == 3:
                src, dst = bufs[3].at[lead], bufs[4]
            else:
                sub = 1 - bits[stage + 1] if turn_of == 0 else bits[stage + 1]
                src, dst = bufs[stage].at[lead, sub], bufs[stage + 1].at[sub]
            self.copies[stage, turn_of] = send(src, dst, *sems)

        def take(self, stage, turn_of):
            bits, bufs = self.bits, self.bufs
            self.copies[stage, turn_of].wait_recv()
            sub = 1 - bits[stage + 1] if turn_of == 0 else bits[stage + 1]
            mine = bufs[stage][bits[stage], sub].astype(jnp.float32)
            bufs[stage + 1][sub] = (
                bufs[stage + 1][sub].astype(jnp.float32) + mine
            ).astype(jnp.bfloat16)
            if turn_of == 0:
                self.launch(stage + 1, 0)
                if stage + 1 < 3:
                    self.launch(stage + 1, 1)

        def finish(self, rows):
            bits, bufs = self.bits, self.bufs
            self.copies[3, 0].wait_recv()
            total = bufs[4][...].astype(jnp.float32) + bufs[3][bits[3]].astype(jnp.float32)
            count = row_count * lax.axis_size("rep") * lax.axis_size("fsdp")
            wg_ref[rows, :] = (total * (1.0 / math.sqrt(count))).astype(jnp.bfloat16)

    fa = Flow(0, (x, y, z0, z1), (over_x, over_y, over_z0, over_z1), (s_a, a1, a2, a3, a4))
    fb = Flow(1, (y, x, z0, z1), (over_y, over_x, over_z0, over_z1), (s_b, b1, b2, b3, b4))

    def use(shard, at):
        col = pl.multiple_of(shard * shard_rows + at * piece, piece)
        cols = pl.ds(col, piece)
        w = wbuf[shard, pl.ds(2 * at, 2)].reshape(piece, width)
        tg_ref[:, cols] = lax.dot_general(
            pg[0], w, (((1,), (1,)), ((), ())), preferred_element_type=jnp.float32
        ).astype(jnp.bfloat16)
        pltpu.make_async_copy(tg_ref.at[:, cols], tg_hbm.at[:, cols], store_sem.at[0]).start()
        proj[...] += jnp.dot(tok_ref[:, cols], w, preferred_element_type=jnp.float32)

    def use_all(shard):
        def one(i, carry):
            use(shard, i)
            return carry

        lax.fori_loop(0, 4, one, 0)

    side = fsdp + 2 - 4 * y
    twin_shard = fsdp + 1 - 2 * c
    twin_side = side + 1 - 2 * c
    there_x, there_z, there = 2 * (1 - x) + z0, 2 * x + 1 - z0, 3 - here
    from_x, from_z, from_twin = [], [], []

    def pass_y(q):
        i = 2 * here + q
        from_y[q].wait_recv()
        from_x.append(send_w(side, i, 2 + q, over_x))
        from_z.append(send_w(side, i, 4 + q, over_z0))
        from_twin.append(send_w(side, i, 8 + q, twin))

    def pass_x(q):
        i = 2 * there_x + q
        from_x[q].wait_recv()
        from_z.append(send_w(side, i, 6 + q, over_z0))
        from_twin.append(send_w(side, i, 10 + q, twin))

    def pass_z(q):
        i = 2 * (there_z if q < 2 else there) + q % 2
        from_z[q].wait_recv()
        from_twin.append(send_w(side, i, 12 + q, twin))

    proj[...] = jnp.zeros_like(proj)
    blocks(1 - x, 1 - y)
    fa.launch(0, 0)
    fb.launch(0, 0)
    pass_y(0)
    blocks(1 - x, y)
    blocks(x, 1 - y)
    pass_y(1)
    fa.launch(0, 1)
    fb.launch(0, 1)
    blocks(x, y)
    use_all(fsdp)
    pass_x(0)
    own.wait_recv()
    use(twin_shard, 0)
    use(twin_shard, 1)
    pass_z(0)
    use(twin_shard, 2)
    use(twin_shard, 3)
    pass_x(1)
    pass_z(1)
    fa.take(0, 0)
    fb.take(0, 0)
    use(side, here)
    pass_z(2)
    use(side, there_x)
    use(side, there_z)
    fb.take(0, 1)
    fa.take(0, 1)
    pass_z(3)
    fa.take(1, 0)
    fb.take(1, 0)
    use(side, there)
    for copy in from_twin[:2]:
        copy.wait_recv()
    use(twin_side, here)
    fa.take(1, 1)
    fb.take(1, 1)
    fa.take(2, 0)
    fb.take(2, 0)
    for copy in from_twin[2:]:
        copy.wait_recv()
    use(twin_side, there_x)
    use(twin_side, there_z)
    fa.take(2, 1)
    fb.take(2, 1)
    use(twin_side, there)
    for h in range(heads):
        cols = slice(h * HEAD_DIM, (h + 1) * HEAD_DIM)
        rot_ref[:, cols] = turn(proj[:, cols], 1.0).astype(jnp.bfloat16)
    fa.finish(slice(0, block // 2))
    fb.finish(slice(block // 2, block))

    pltpu.make_async_copy(tg_ref, tg_hbm, store_sem.at[0]).wait()
    all_tokens.wait_send()
    for copy in started:
        copy.wait_send()


def fused_body(tokens, quant_weight, block_scales, key_grad):
    row_count, model = tokens.shape
    shard_rows, width = quant_weight.shape
    block = model // (lax.axis_size("rep") * lax.axis_size("fsdp"))
    bf16, f32 = jnp.bfloat16, jnp.float32
    vmem = pl.BlockSpec(memory_space=pltpu.VMEM)
    hbm = pl.BlockSpec(memory_space=pltpu.HBM)
    flows = [
        pltpu.VMEM((2,) * (4 - level) + (block // 2, width), bf16)
        for level in range(5)
        for _ in range(2)
    ]
    return pl.pallas_call(
        fused_kernel,
        out_shape=[
            jax.ShapeDtypeStruct((row_count, width), bf16),
            jax.ShapeDtypeStruct((row_count, model), bf16),
            jax.ShapeDtypeStruct((block, width), bf16),
        ],
        in_specs=[hbm, hbm, vmem, hbm],
        out_specs=[vmem, hbm, vmem],
        scratch_shapes=[
            pltpu.VMEM((row_count, model), bf16),
            pltpu.VMEM((shard_rows, width), bf16),
            pltpu.VMEM((row_count, width), bf16),
            pltpu.VMEM((row_count, model), bf16),
            pltpu.VMEM((4, 8, shard_rows // 8, width), bf16),
            pltpu.VMEM((16, row_count, block), bf16),
            pltpu.VMEM((2, row_count, width), bf16),
            pltpu.VMEM((row_count, width), f32),
            pltpu.VMEM((row_count, HEAD_DIM), f32),
            pltpu.VMEM((row_count, HEAD_DIM), f32),
            *flows,
            pltpu.SemaphoreType.DMA((3,)),
            pltpu.SemaphoreType.DMA((1,)),
            pltpu.SemaphoreType.DMA((2,)),
            pltpu.SemaphoreType.DMA((2,)),
            pltpu.SemaphoreType.DMA((17,)),
            pltpu.SemaphoreType.DMA((17,)),
            pltpu.SemaphoreType.DMA((16,)),
            pltpu.SemaphoreType.DMA((16,)),
        ],
        compiler_params=pltpu.CompilerParams(
            collective_id=0, has_side_effects=True, vmem_limit_bytes=56 * 1024 * 1024
        ),
    )(tokens, quant_weight, block_scales.reshape(1, -1), key_grad)


def solution(mesh):
    paired = mesh.shape["rep"] == 8 and mesh.shape["fsdp"] == 4
    return jax.shard_map(
        fused_body if paired else body,
        mesh=mesh,
        in_specs=(P(("rep", "fsdp"), None), P("fsdp", None), P("fsdp"), P(("rep", "fsdp"), None)),
        out_specs=(P(("rep", "fsdp"), None), P(("rep", "fsdp"), None), P(("rep", "fsdp"), None)),
        check_vma=False,
    )
```

```python
import math

import jax
import jax.numpy as jnp
from jax import lax
from jax.experimental import pallas as pl
from jax.experimental.pallas import tpu as pltpu
from jax.sharding import PartitionSpec as P

HEAD_DIM = 128


rope_base = 10000.0


def dequantize(quant_weight, block_scales):
    rows_per_block = quant_weight.shape[0] // block_scales.shape[0]
    scaled = quant_weight.astype(jnp.float32).reshape(
        block_scales.shape[0], rows_per_block, quant_weight.shape[1]
    )
    scaled = scaled * block_scales.astype(jnp.float32)[:, None, None]
    return scaled.reshape(quant_weight.shape).astype(jnp.bfloat16)


def rotary(projected, positions, direction):
    half_size = HEAD_DIM // 2
    steps = jnp.arange(half_size, dtype=jnp.int32).astype(jnp.float32)
    frequency = jnp.exp(steps * (-2.0 * math.log(rope_base) / HEAD_DIM))
    angles = positions[:, None] * frequency[None, :]
    cosine = jnp.cos(angles)[:, None, :]
    sine_part = direction * jnp.sin(angles)[:, None, :]
    halves = projected.reshape(projected.shape[0], -1, 2, half_size)
    leading = halves[:, :, 0]
    trailing = halves[:, :, 1]
    turned = jnp.stack(
        [leading * cosine - trailing * sine_part, trailing * cosine + leading * sine_part], axis=2
    )
    return turned.reshape(projected.shape)


def partial_rows(source, proj_grad):
    return lax.dot_general(
        source, proj_grad, (((0,), (0,)), ((), ())), preferred_element_type=jnp.float32
    )


def body(tokens, quant_weight, block_scales, key_grad):
    row_count = tokens.shape[0]
    all_codes, all_scales = (
        lax.all_gather(quant_weight, "fsdp", axis=0, tiled=True),
        lax.all_gather(block_scales, "fsdp", axis=0, tiled=True),
    )
    weight = dequantize(all_codes, all_scales)
    positions = (
        lax.axis_index("fsdp") * row_count + jnp.arange(row_count, dtype=jnp.int32)
    ).astype(jnp.float32)
    projected = jnp.dot(tokens, weight, preferred_element_type=jnp.float32)
    rotated = rotary(projected, positions, 1.0).astype(jnp.bfloat16)
    proj_grad = rotary(key_grad.astype(jnp.float32), positions, -1.0).astype(jnp.bfloat16)
    token_grad = lax.dot_general(
        proj_grad, weight, (((1,), (1,)), ((), ())), preferred_element_type=jnp.float32
    ).astype(jnp.bfloat16)
    total_rows = weight.shape[0]
    fsdp_size = lax.axis_size("fsdp")
    rep_size = lax.axis_size("rep")
    share = total_rows // (fsdp_size * rep_size)
    reordered = (
        tokens.reshape(row_count, rep_size, fsdp_size, share)
        .transpose(0, 2, 1, 3)
        .reshape(row_count, total_rows)
    )
    group_sum = lax.psum_scatter(
        partial_rows(reordered, proj_grad).astype(jnp.bfloat16),
        "fsdp",
        scatter_dimension=0,
        tiled=True,
    ).astype(jnp.float32)
    summed = lax.psum_scatter(group_sum, "rep", scatter_dimension=0, tiled=True)
    weight_grad = (summed * (1.0 / math.sqrt(row_count * fsdp_size * rep_size))).astype(
        jnp.bfloat16
    )
    return (rotated, token_grad, weight_grad)


MESH = pl.DeviceIdType.MESH


def fused_kernel(
    tok_hbm, quant_hbm, scale_ref, kg_hbm,
    rot_ref, tg_hbm, wg_ref,
    tok_ref, quant_ref, kg_ref, tg_ref,
    wbuf, tok_twin, pg, proj, cos_t, sin_t,
    sa, sb, sc, sd, a1, b1, c1, d1, a2, b2, c2, d2, a3, b3, c3, d3, a4, b4, c4, d4,
    load_sem, store_sem, tok_sem, pg_sem, w_send, w_recv, rs_send, rs_recv,
):
    rep, fsdp = lax.axis_index("rep"), lax.axis_index("fsdp")
    x, z0, z1 = rep % 2, (rep // 2) % 2, rep // 4
    y, c = fsdp // 2, fsdp % 2
    twin = (rep, fsdp + 1 - 2 * c)
    over_y = (rep, fsdp + 2 - 4 * y)
    over_x = (rep + 1 - 2 * x, fsdp)
    over_z0 = (rep + 2 - 4 * z0, fsdp)
    over_z1 = (rep + 4 - 8 * z1, fsdp)
    row_count, width = kg_ref.shape
    shard_rows = quant_ref.shape[0]
    piece = shard_rows // 4
    part = shard_rows // 8
    block = wg_ref.shape[0]
    here = 2 * x + z0

    load_quant = pltpu.make_async_copy(quant_hbm, quant_ref, load_sem.at[0])
    load_quant.start()
    load_kg = pltpu.make_async_copy(kg_hbm, kg_ref, load_sem.at[1])
    load_kg.start()
    load_tok = pltpu.make_async_copy(tok_hbm, tok_ref, load_sem.at[2])
    load_tok.start()

    barrier = pltpu.get_barrier_semaphore()
    for other in (twin, over_y, over_x, over_z0, over_z1):
        pl.semaphore_signal(barrier, inc=1, device_id=other, device_id_type=MESH)

    def dequant(i):
        rows = pl.ds(pl.multiple_of(i * part, part), part)
        n_blocks = scale_ref.shape[1]
        per_block = shard_rows // n_blocks
        owner = (i * part + lax.broadcasted_iota(jnp.int32, (part, n_blocks), 0)) // per_block
        lane = lax.broadcasted_iota(jnp.int32, (part, n_blocks), 1)
        picked = jnp.where(owner == lane, scale_ref[...].astype(jnp.float32), 0.0)
        column = jnp.sum(picked, axis=1, keepdims=True)
        wbuf[fsdp, i] = (quant_ref[rows, :].astype(jnp.float32) * column).astype(jnp.bfloat16)

    load_quant.wait()
    dequant(2 * here)
    dequant(2 * here + 1)
    pl.semaphore_wait(barrier, 5)

    started = []

    def send(src, dst, send_sem, recv_sem, to):
        copy = pltpu.make_async_remote_copy(
            src_ref=src, dst_ref=dst, send_sem=send_sem, recv_sem=recv_sem,
            device_id=to, device_id_type=MESH,
        )
        copy.start()
        started.append(copy)
        return copy

    def send_w(shard, i, slot, to):
        return send(
            wbuf.at[shard, i], wbuf.at[shard, i], w_send.at[slot], w_recv.at[slot], to
        )

    from_y = [send_w(fsdp, 2 * here + q, q, over_y) for q in range(2)]

    def send_tokens(j, carry):
        col = pl.multiple_of((2 * j + 1 - c) * block, block)
        pltpu.make_async_remote_copy(
            src_ref=tok_hbm.at[:, pl.ds(col, block)], dst_ref=tok_twin.at[j],
            send_sem=tok_sem.at[0], recv_sem=tok_sem.at[1],
            device_id=twin, device_id_type=MESH,
        ).start()
        return carry

    lax.fori_loop(0, 16, send_tokens, 0)
    all_tokens = pltpu.make_async_remote_copy(
        src_ref=tok_twin, dst_ref=tok_twin, send_sem=tok_sem.at[0], recv_sem=tok_sem.at[1],
        device_id=twin, device_id_type=MESH,
    )

    half = HEAD_DIM // 2
    low_rows = 8
    high_rows = row_count // low_rows

    def angles(rows, first, step):
        shape = (rows, HEAD_DIM)
        steps = (lax.broadcasted_iota(jnp.int32, shape, 1) % half).astype(jnp.float32)
        frequency = jnp.exp(steps * (-2.0 * math.log(rope_base) / HEAD_DIM))
        place = first + step * lax.broadcasted_iota(jnp.int32, shape, 0)
        return place.astype(jnp.float32) * frequency

    high = angles(high_rows, fsdp * row_count, low_rows)
    low = angles(low_rows, 0, 1)
    cos_high, sin_high = jnp.cos(high), jnp.sin(high)
    cos_low, sin_low = jnp.cos(low), jnp.sin(low)
    leading = lax.broadcasted_iota(jnp.int32, (low_rows, HEAD_DIM), 1) < half
    for i in range(high_rows):
        rows = slice(i * low_rows, (i + 1) * low_rows)
        ch, sh = cos_high[i : i + 1], sin_high[i : i + 1]
        cos_t[rows, :] = ch * cos_low - sh * sin_low
        sine = sh * cos_low + ch * sin_low
        sin_t[rows, :] = jnp.where(leading, -sine, sine)

    def turn(value, direction):
        return value * cos_t[...] + pltpu.roll(value, half, 1) * (direction * sin_t[...])

    heads = width // HEAD_DIM
    load_kg.wait()
    for h in range(heads):
        cols = slice(h * HEAD_DIM, (h + 1) * HEAD_DIM)
        pg[0, :, cols] = turn(kg_ref[:, cols].astype(jnp.float32), -1.0).astype(jnp.bfloat16)
    pg_copy = send(pg.at[0], pg.at[1], pg_sem.at[0], pg_sem.at[1], twin)

    load_tok.wait()
    all_tokens.wait_recv()
    pg_copy.wait_recv()

    quarter = block // 4

    def blocks(bx, by):
        def one(bz, carry):
            bz0, bz1 = bz // 2, bz % 2
            index = bz1 * 8 + bz0 * 4 + bx * 2 + by
            col = pl.multiple_of((2 * index + c) * block, block)
            left = jnp.concatenate([tok_ref[:, pl.ds(col, block)], tok_twin[index]], axis=0)
            right = pg[...].reshape(2 * row_count, width)
            total = lax.dot_general(
                left, right, (((0,), (0,)), ((), ())), preferred_element_type=jnp.float32
            ).astype(jnp.bfloat16)
            sa[bx, by, bz0, bz1] = total[:quarter]
            sb[by, bx, bz0, bz1] = total[quarter : 2 * quarter]
            sc[bx, by, bz0, bz1] = total[2 * quarter : 3 * quarter]
            sd[by, bx, bz0, bz1] = total[3 * quarter :]
            return carry

        lax.fori_loop(0, 4, one, 0)

    class Flow:
        def __init__(self, index, bits, others, bufs):
            self.index, self.bits, self.others, self.bufs = index, bits, others, bufs
            self.copies = {}

        def launch(self, stage, turn_of):
            bits, bufs = self.bits, self.bufs
            slot = self.index * 8 + stage * 2 + turn_of
            sems = (rs_send.at[slot], rs_recv.at[slot], self.others[stage])
            lead = 1 - bits[stage]
            if stage == 3:
                src, dst = bufs[3].at[lead], bufs[4]
            else:
                sub = 1 - bits[stage + 1] if turn_of == 0 else bits[stage + 1]
                src, dst = bufs[stage].at[lead, sub], bufs[stage + 1].at[sub]
            self.copies[stage, turn_of] = send(src, dst, *sems)

        def take(self, stage, turn_of):
            bits, bufs = self.bits, self.bufs
            self.copies[stage, turn_of].wait_recv()
            sub = 1 - bits[stage + 1] if turn_of == 0 else bits[stage + 1]
            mine = bufs[stage][bits[stage], sub].astype(jnp.float32)
            bufs[stage + 1][sub] = (
                bufs[stage + 1][sub].astype(jnp.float32) + mine
            ).astype(jnp.bfloat16)
            if turn_of == 0:
                self.launch(stage + 1, 0)
                if stage + 1 < 3:
                    self.launch(stage + 1, 1)

        def finish(self, rows):
            bits, bufs = self.bits, self.bufs
            self.copies[3, 0].wait_recv()
            total = bufs[4][...].astype(jnp.float32) + bufs[3][bits[3]].astype(jnp.float32)
            count = row_count * lax.axis_size("rep") * lax.axis_size("fsdp")
            wg_ref[rows, :] = (total * (1.0 / math.sqrt(count))).astype(jnp.bfloat16)

    x_first = ((x, y, z0, z1), (over_x, over_y, over_z0, over_z1))
    y_first = ((y, x, z0, z1), (over_y, over_x, over_z0, over_z1))
    fa = Flow(0, *x_first, (sa, a1, a2, a3, a4))
    fb = Flow(1, *y_first, (sb, b1, b2, b3, b4))
    fc = Flow(2, *x_first, (sc, c1, c2, c3, c4))
    fd = Flow(3, *y_first, (sd, d1, d2, d3, d4))

    def use(shard, at):
        col = pl.multiple_of(shard * shard_rows + at * piece, piece)
        cols = pl.ds(col, piece)
        w = wbuf[shard, pl.ds(2 * at, 2)].reshape(piece, width)
        tg_ref[:, cols] = lax.dot_general(
            pg[0], w, (((1,), (1,)), ((), ())), preferred_element_type=jnp.float32
        ).astype(jnp.bfloat16)
        pltpu.make_async_copy(tg_ref.at[:, cols], tg_hbm.at[:, cols], store_sem.at[0]).start()
        proj[...] += jnp.dot(tok_ref[:, cols], w, preferred_element_type=jnp.float32)

    def use_all(shard):
        def one(i, carry):
            use(shard, i)
            return carry

        lax.fori_loop(0, 4, one, 0)

    side = fsdp + 2 - 4 * y
    twin_shard = fsdp + 1 - 2 * c
    twin_side = side + 1 - 2 * c
    there_x, there_z, there = 2 * (1 - x) + z0, 2 * x + 1 - z0, 3 - here
    from_x, from_z, from_twin = [], [], []

    def pass_y(q):
        i = 2 * here + q
        from_y[q].wait_recv()
        from_x.append(send_w(side, i, 2 + q, over_x))
        from_z.append(send_w(side, i, 4 + q, over_z0))
        from_twin.append(send_w(side, i, 8 + q, twin))

    def pass_x(q):
        i = 2 * there_x + q
        from_x[q].wait_recv()
        from_z.append(send_w(side, i, 6 + q, over_z0))
        from_twin.append(send_w(side, i, 10 + q, twin))

    def pass_z(q):
        i = 2 * (there_z if q < 2 else there) + q % 2
        from_z[q].wait_recv()
        from_twin.append(send_w(side, i, 12 + q, twin))

    proj[...] = jnp.zeros_like(proj)
    blocks(1 - x, 1 - y)
    fa.launch(0, 0)
    fb.launch(0, 0)
    pass_y(0)
    blocks(1 - x, y)
    blocks(x, 1 - y)
    fa.launch(0, 1)
    fb.launch(0, 1)
    pass_y(1)
    blocks(x, y)
    def dequant_other(i, carry):
        other = (2 * here + 2 + i) % 8
        dequant(other)
        return carry

    lax.fori_loop(0, 6, dequant_other, 0)
    own = send(wbuf.at[fsdp], wbuf.at[fsdp], w_send.at[16], w_recv.at[16], twin)
    use_all(fsdp)
    pass_x(0)
    fa.take(0, 0)
    fb.take(0, 0)
    for turn_of in range(2):
        fc.launch(0, turn_of)
        fd.launch(0, turn_of)
    pass_z(0)
    pass_x(1)
    own.wait_recv()
    use(twin_shard, 0)
    use(twin_shard, 1)
    pass_z(1)
    fa.take(0, 1)
    fb.take(0, 1)
    use(twin_shard, 2)
    use(twin_shard, 3)
    fa.take(1, 0)
    fb.take(1, 0)
    use(side, here)
    pass_z(2)
    fc.take(0, 0)
    fd.take(0, 0)
    fa.take(1, 1)
    fb.take(1, 1)
    pass_z(3)
    use(side, there_x)
    use(side, there_z)
    fa.take(2, 0)
    fb.take(2, 0)
    fc.take(0, 1)
    fd.take(0, 1)
    use(side, there)
    for copy in from_twin[:2]:
        copy.wait_recv()
    use(twin_side, here)
    fc.take(1, 0)
    fd.take(1, 0)
    fa.take(2, 1)
    fb.take(2, 1)
    for copy in from_twin[2:]:
        copy.wait_recv()
    use(twin_side, there_x)
    use(twin_side, there_z)
    fc.take(1, 1)
    fd.take(1, 1)
    use(twin_side, there)
    fc.take(2, 0)
    fd.take(2, 0)
    for h in range(heads):
        cols = slice(h * HEAD_DIM, (h + 1) * HEAD_DIM)
        rot_ref[:, cols] = turn(proj[:, cols], 1.0).astype(jnp.bfloat16)
    fa.finish(slice(0, quarter))
    fb.finish(slice(quarter, 2 * quarter))
    fc.take(2, 1)
    fd.take(2, 1)
    fc.finish(slice(2 * quarter, 3 * quarter))
    fd.finish(slice(3 * quarter, block))

    pltpu.make_async_copy(tg_ref, tg_hbm, store_sem.at[0]).wait()
    all_tokens.wait_send()
    for copy in started:
        copy.wait_send()


def fused_body(tokens, quant_weight, block_scales, key_grad):
    row_count, model = tokens.shape
    shard_rows, width = quant_weight.shape
    block = model // (lax.axis_size("rep") * lax.axis_size("fsdp"))
    bf16, f32 = jnp.bfloat16, jnp.float32
    vmem = pl.BlockSpec(memory_space=pltpu.VMEM)
    hbm = pl.BlockSpec(memory_space=pltpu.HBM)
    flows = [
        pltpu.VMEM((2,) * (4 - level) + (block // 4, width), bf16)
        for level in range(5)
        for _ in range(4)
    ]
    results = pl.pallas_call(
        fused_kernel,
        out_shape=[
            jax.ShapeDtypeStruct((row_count, width), bf16),
            jax.ShapeDtypeStruct((row_count, model), bf16),
            jax.ShapeDtypeStruct((block, width), bf16),
        ],
        in_specs=[hbm, hbm, vmem, hbm],
        out_specs=[vmem, hbm, vmem],
        scratch_shapes=[
            pltpu.VMEM((row_count, model), bf16),
            pltpu.VMEM((shard_rows, width), bf16),
            pltpu.VMEM((row_count, width), bf16),
            pltpu.VMEM((row_count, model), bf16),
            pltpu.VMEM((4, 8, shard_rows // 8, width), bf16),
            pltpu.VMEM((16, row_count, block), bf16),
            pltpu.VMEM((2, row_count, width), bf16),
            pltpu.VMEM((row_count, width), f32),
            pltpu.VMEM((row_count, HEAD_DIM), f32),
            pltpu.VMEM((row_count, HEAD_DIM), f32),
            *flows,
            pltpu.SemaphoreType.DMA((3,)),
            pltpu.SemaphoreType.DMA((1,)),
            pltpu.SemaphoreType.DMA((2,)),
            pltpu.SemaphoreType.DMA((2,)),
            pltpu.SemaphoreType.DMA((17,)),
            pltpu.SemaphoreType.DMA((17,)),
            pltpu.SemaphoreType.DMA((32,)),
            pltpu.SemaphoreType.DMA((32,)),
        ],
        compiler_params=pltpu.CompilerParams(
            collective_id=0, has_side_effects=True, vmem_limit_bytes=56 * 1024 * 1024
        ),
    )(tokens, quant_weight, block_scales.reshape(1, -1), key_grad)
    return pl.pallas_call(
        place_kernel,
        out_shape=[jax.ShapeDtypeStruct(value.shape, value.dtype) for value in results],
        in_specs=[hbm] * 3,
        out_specs=[hbm] * 3,
        scratch_shapes=[pltpu.SemaphoreType.DMA((6,))],
    )(*results)


def place_kernel(rot_in, tg_in, wg_in, rot_out, tg_out, wg_out, sems):
    rows = tg_in.shape[0] // 4
    copies = [
        pltpu.make_async_copy(
            tg_in.at[pl.ds(i * rows, rows)], tg_out.at[pl.ds(i * rows, rows)], sems.at[i]
        )
        for i in range(4)
    ]
    copies.append(pltpu.make_async_copy(rot_in, rot_out, sems.at[4]))
    copies.append(pltpu.make_async_copy(wg_in, wg_out, sems.at[5]))
    for copy in copies:
        copy.start()
    for copy in copies:
        copy.wait()


def solution(mesh):
    paired = mesh.shape["rep"] == 8 and mesh.shape["fsdp"] == 4
    return jax.shard_map(
        fused_body if paired else body,
        mesh=mesh,
        in_specs=(P(("rep", "fsdp"), None), P("fsdp", None), P("fsdp"), P(("rep", "fsdp"), None)),
        out_specs=(P(("rep", "fsdp"), None), P(("rep", "fsdp"), None), P(("rep", "fsdp"), None)),
        check_vma=False,
    )
```

```python
import math

import jax
import jax.numpy as jnp
from jax import lax
from jax.experimental import pallas as pl
from jax.experimental.pallas import tpu as pltpu
from jax.sharding import PartitionSpec as P

HEAD_DIM = 128


rope_base = 10000.0


def dequantize(quant_weight, block_scales):
    rows_per_block = quant_weight.shape[0] // block_scales.shape[0]
    scaled = quant_weight.astype(jnp.float32).reshape(
        block_scales.shape[0], rows_per_block, quant_weight.shape[1]
    )
    scaled = scaled * block_scales.astype(jnp.float32)[:, None, None]
    return scaled.reshape(quant_weight.shape).astype(jnp.bfloat16)


def rotary(projected, positions, direction):
    half_size = HEAD_DIM // 2
    steps = jnp.arange(half_size, dtype=jnp.int32).astype(jnp.float32)
    frequency = jnp.exp(steps * (-2.0 * math.log(rope_base) / HEAD_DIM))
    angles = positions[:, None] * frequency[None, :]
    cosine = jnp.cos(angles)[:, None, :]
    sine_part = direction * jnp.sin(angles)[:, None, :]
    halves = projected.reshape(projected.shape[0], -1, 2, half_size)
    leading = halves[:, :, 0]
    trailing = halves[:, :, 1]
    turned = jnp.stack(
        [leading * cosine - trailing * sine_part, trailing * cosine + leading * sine_part], axis=2
    )
    return turned.reshape(projected.shape)


def partial_rows(source, proj_grad):
    return lax.dot_general(
        source, proj_grad, (((0,), (0,)), ((), ())), preferred_element_type=jnp.float32
    )


def body(tokens, quant_weight, block_scales, key_grad):
    row_count = tokens.shape[0]
    all_codes, all_scales = (
        lax.all_gather(quant_weight, "fsdp", axis=0, tiled=True),
        lax.all_gather(block_scales, "fsdp", axis=0, tiled=True),
    )
    weight = dequantize(all_codes, all_scales)
    positions = (
        lax.axis_index("fsdp") * row_count + jnp.arange(row_count, dtype=jnp.int32)
    ).astype(jnp.float32)
    projected = jnp.dot(tokens, weight, preferred_element_type=jnp.float32)
    rotated = rotary(projected, positions, 1.0).astype(jnp.bfloat16)
    proj_grad = rotary(key_grad.astype(jnp.float32), positions, -1.0).astype(jnp.bfloat16)
    token_grad = lax.dot_general(
        proj_grad, weight, (((1,), (1,)), ((), ())), preferred_element_type=jnp.float32
    ).astype(jnp.bfloat16)
    total_rows = weight.shape[0]
    fsdp_size = lax.axis_size("fsdp")
    rep_size = lax.axis_size("rep")
    share = total_rows // (fsdp_size * rep_size)
    reordered = (
        tokens.reshape(row_count, rep_size, fsdp_size, share)
        .transpose(0, 2, 1, 3)
        .reshape(row_count, total_rows)
    )
    group_sum = lax.psum_scatter(
        partial_rows(reordered, proj_grad).astype(jnp.bfloat16),
        "fsdp",
        scatter_dimension=0,
        tiled=True,
    ).astype(jnp.float32)
    summed = lax.psum_scatter(group_sum, "rep", scatter_dimension=0, tiled=True)
    weight_grad = (summed * (1.0 / math.sqrt(row_count * fsdp_size * rep_size))).astype(
        jnp.bfloat16
    )
    return (rotated, token_grad, weight_grad)


MESH = pl.DeviceIdType.MESH


def fused_kernel(
    tok_hbm, quant_hbm, scale_ref, kg_hbm,
    rot_ref, tg_ref, wg_ref,
    tok_ref, quant_ref, kg_ref,
    wbuf, tok_twin, pg, proj, cos_t, sin_t,
    sa, sb, sc, sd, a1, b1, c1, d1, a2, b2, c2, d2, a3, b3, c3, d3, a4, b4, c4, d4,
    load_sem, tok_sem, pg_sem, w_send, w_recv, rs_send, rs_recv,
):
    rep, fsdp = lax.axis_index("rep"), lax.axis_index("fsdp")
    x, z0, z1 = rep % 2, (rep // 2) % 2, rep // 4
    y, c = fsdp // 2, fsdp % 2
    twin = (rep, fsdp + 1 - 2 * c)
    over_y = (rep, fsdp + 2 - 4 * y)
    over_x = (rep + 1 - 2 * x, fsdp)
    over_z0 = (rep + 2 - 4 * z0, fsdp)
    over_z1 = (rep + 4 - 8 * z1, fsdp)
    row_count, width = kg_ref.shape
    shard_rows = quant_ref.shape[0]
    piece = shard_rows // 4
    part = shard_rows // 8
    block = wg_ref.shape[0]
    here = 2 * x + z0

    load_quant = pltpu.make_async_copy(quant_hbm, quant_ref, load_sem.at[0])
    load_quant.start()
    load_kg = pltpu.make_async_copy(kg_hbm, kg_ref, load_sem.at[1])
    load_kg.start()
    load_tok = pltpu.make_async_copy(tok_hbm, tok_ref, load_sem.at[2])
    load_tok.start()

    barrier = pltpu.get_barrier_semaphore()
    for other in (twin, over_y, over_x, over_z0, over_z1):
        pl.semaphore_signal(barrier, inc=1, device_id=other, device_id_type=MESH)

    def dequant(i):
        rows = pl.ds(pl.multiple_of(i * part, part), part)
        n_blocks = scale_ref.shape[0]
        per_block = shard_rows // n_blocks
        owner = (i * part + lax.broadcasted_iota(jnp.int32, (part, n_blocks), 0)) // per_block
        lane = lax.broadcasted_iota(jnp.int32, (part, n_blocks), 1)
        picked = jnp.where(owner == lane, scale_ref[...].astype(jnp.float32).reshape(1, n_blocks), 0.0)
        column = jnp.sum(picked, axis=1, keepdims=True)
        wbuf[fsdp, i] = (quant_ref[rows, :].astype(jnp.float32) * column).astype(jnp.bfloat16)

    half = HEAD_DIM // 2
    low_rows = 8
    high_rows = row_count // low_rows

    def angles(rows, first, step):
        shape = (rows, HEAD_DIM)
        steps = (lax.broadcasted_iota(jnp.int32, shape, 1) % half).astype(jnp.float32)
        frequency = jnp.exp(steps * (-2.0 * math.log(rope_base) / HEAD_DIM))
        place = first + step * lax.broadcasted_iota(jnp.int32, shape, 0)
        return place.astype(jnp.float32) * frequency

    high = angles(high_rows, fsdp * row_count, low_rows)
    low = angles(low_rows, 0, 1)
    cos_high, sin_high = jnp.cos(high), jnp.sin(high)
    cos_low, sin_low = jnp.cos(low), jnp.sin(low)
    leading = lax.broadcasted_iota(jnp.int32, (low_rows, HEAD_DIM), 1) < half
    for i in range(high_rows):
        rows = slice(i * low_rows, (i + 1) * low_rows)
        ch, sh = cos_high[i : i + 1], sin_high[i : i + 1]
        cos_t[rows, :] = ch * cos_low - sh * sin_low
        sine = sh * cos_low + ch * sin_low
        sin_t[rows, :] = jnp.where(leading, -sine, sine)

    def turn(value, direction):
        return value * cos_t[...] + pltpu.roll(value, half, 1) * (direction * sin_t[...])

    heads = width // HEAD_DIM
    load_kg.wait()
    for h in range(heads):
        cols = slice(h * HEAD_DIM, (h + 1) * HEAD_DIM)
        pg[0, :, cols] = turn(kg_ref[:, cols].astype(jnp.float32), -1.0).astype(jnp.bfloat16)
    load_quant.wait()
    dequant(2 * here)
    dequant(2 * here + 1)
    pl.semaphore_wait(barrier, 5)

    started = []

    def send(src, dst, send_sem, recv_sem, to):
        copy = pltpu.make_async_remote_copy(
            src_ref=src, dst_ref=dst, send_sem=send_sem, recv_sem=recv_sem,
            device_id=to, device_id_type=MESH,
        )
        copy.start()
        started.append(copy)
        return copy

    def send_w(shard, i, slot, to):
        return send(
            wbuf.at[shard, i], wbuf.at[shard, i], w_send.at[slot], w_recv.at[slot], to
        )

    from_y = [send_w(fsdp, 2 * here + q, q, over_y) for q in range(2)]

    def send_tokens(bx, by):
        group = 2 * bx + by
        for k in range(4):
            col = pl.multiple_of(((k % 2 * 8 + k // 2 * 4 + group) * 2 + 1 - c) * block, block)
            pltpu.make_async_remote_copy(
                src_ref=tok_ref.at[:, pl.ds(col, block)],
                dst_ref=tok_twin.at[bx, by, :, pl.ds(k * block, block)],
                send_sem=tok_sem.at[group], recv_sem=tok_sem.at[4 + group],
                device_id=twin, device_id_type=MESH,
            ).start()

    def group_copy(bx, by):
        group = 2 * bx + by
        return pltpu.make_async_remote_copy(
            src_ref=tok_twin.at[bx, by], dst_ref=tok_twin.at[bx, by],
            send_sem=tok_sem.at[group], recv_sem=tok_sem.at[4 + group],
            device_id=twin, device_id_type=MESH,
        )

    load_tok.wait()
    send_tokens(1 - x, 1 - y)
    pg_copy = send(pg.at[0], pg.at[1], pg_sem.at[0], pg_sem.at[1], twin)
    send_tokens(1 - x, y)
    send_tokens(x, 1 - y)
    send_tokens(x, y)
    pg_copy.wait_recv()

    quarter = block // 4

    def blocks(bx, by):
        group_copy(bx, by).wait_recv()
        own_columns = [
            tok_ref[:, pl.ds(pl.multiple_of(((k % 2 * 8 + k // 2 * 4 + 2 * bx + by) * 2 + c) * block, block), block)]
            for k in range(4)
        ]
        left = jnp.concatenate(
            [jnp.concatenate(own_columns, axis=1), tok_twin[bx, by]], axis=0
        )
        right = pg[...].reshape(2 * row_count, width)
        total = lax.dot_general(
            left, right, (((0,), (0,)), ((), ())), preferred_element_type=jnp.float32
        ).astype(jnp.bfloat16).reshape(2, 2, 4, quarter, width)
        sa[bx, by] = total[:, :, 0]
        sb[by, bx] = total[:, :, 1]
        for bz0 in range(2):
            sc[bx, bz0, by] = total[bz0, :, 2]
            sd[by, bz0, bx] = total[bz0, :, 3]

    class Flow:
        def __init__(self, index, bits, others, bufs):
            self.index, self.bits, self.others, self.bufs = index, bits, others, bufs
            self.copies = {}

        def launch(self, stage, turn_of):
            bits, bufs = self.bits, self.bufs
            slot = self.index * 8 + stage * 2 + turn_of
            sems = (rs_send.at[slot], rs_recv.at[slot], self.others[stage])
            lead = 1 - bits[stage]
            if stage == 3:
                src, dst = bufs[3].at[lead], bufs[4]
            else:
                sub = 1 - bits[stage + 1] if turn_of == 0 else bits[stage + 1]
                src, dst = bufs[stage].at[lead, sub], bufs[stage + 1].at[sub]
            self.copies[stage, turn_of] = send(src, dst, *sems)

        def take(self, stage, turn_of):
            bits, bufs = self.bits, self.bufs
            self.copies[stage, turn_of].wait_recv()
            sub = 1 - bits[stage + 1] if turn_of == 0 else bits[stage + 1]
            mine = bufs[stage][bits[stage], sub].astype(jnp.float32)
            bufs[stage + 1][sub] = (
                bufs[stage + 1][sub].astype(jnp.float32) + mine
            ).astype(jnp.bfloat16)
            if turn_of == 0:
                self.launch(stage + 1, 0)
                if stage + 1 < 3:
                    self.launch(stage + 1, 1)

        def finish(self, rows):
            bits, bufs = self.bits, self.bufs
            self.copies[3, 0].wait_recv()
            total = bufs[4][...].astype(jnp.float32) + bufs[3][bits[3]].astype(jnp.float32)
            count = row_count * lax.axis_size("rep") * lax.axis_size("fsdp")
            wg_ref[rows, :] = (total * (1.0 / math.sqrt(count))).astype(jnp.bfloat16)

    x_first = ((x, y, z0, z1), (over_x, over_y, over_z0, over_z1))
    y_first = ((y, x, z0, z1), (over_y, over_x, over_z0, over_z1))
    fa = Flow(0, *x_first, (sa, a1, a2, a3, a4))
    fb = Flow(1, *y_first, (sb, b1, b2, b3, b4))
    x_then_z = ((x, z0, y, z1), (over_x, over_z0, over_y, over_z1))
    y_then_z = ((y, z0, x, z1), (over_y, over_z0, over_x, over_z1))
    fc = Flow(2, *x_then_z, (sc, c1, c2, c3, c4))
    fd = Flow(3, *y_then_z, (sd, d1, d2, d3, d4))

    def use(shard, at):
        col = pl.multiple_of(shard * shard_rows + at * piece, piece)
        cols = pl.ds(col, piece)
        w = wbuf[shard, pl.ds(2 * at, 2)].reshape(piece, width)
        tg_ref[:, cols] = lax.dot_general(
            pg[0], w, (((1,), (1,)), ((), ())), preferred_element_type=jnp.float32
        ).astype(jnp.bfloat16)
        proj[...] += jnp.dot(tok_ref[:, cols], w, preferred_element_type=jnp.float32)

    def use_all(shard):
        def one(i, carry):
            use(shard, i)
            return carry

        lax.fori_loop(0, 4, one, 0)

    side = fsdp + 2 - 4 * y
    twin_shard = fsdp + 1 - 2 * c
    twin_side = side + 1 - 2 * c
    there_x, there_z, there = 2 * (1 - x) + z0, 2 * x + 1 - z0, 3 - here
    from_x, from_z, from_twin = [], [], []

    def pass_y(q):
        i = 2 * here + q
        from_y[q].wait_recv()
        from_x.append(send_w(side, i, 2 + q, over_x))
        from_z.append(send_w(side, i, 4 + q, over_z0))
        from_twin.append(send_w(side, i, 8 + q, twin))

    def pass_x(q):
        i = 2 * there_x + q
        from_x[q].wait_recv()
        from_z.append(send_w(side, i, 6 + q, over_z0))
        from_twin.append(send_w(side, i, 10 + q, twin))

    def pass_z(q):
        i = 2 * (there_z if q < 2 else there) + q % 2
        from_z[q].wait_recv()
        from_twin.append(send_w(side, i, 12 + q, twin))

    proj[...] = jnp.zeros_like(proj)
    blocks(1 - x, 1 - y)
    fa.launch(0, 0)
    fb.launch(0, 0)
    pass_y(0)
    blocks(1 - x, y)
    blocks(x, 1 - y)
    fa.launch(0, 1)
    fb.launch(0, 1)
    pass_y(1)
    blocks(x, y)
    def dequant_other(i, carry):
        other = (2 * here + 2 + i) % 8
        dequant(other)
        return carry

    lax.fori_loop(0, 6, dequant_other, 0)
    own = send(wbuf.at[fsdp], wbuf.at[fsdp], w_send.at[16], w_recv.at[16], twin)
    use_all(fsdp)
    pass_x(0)
    fa.take(0, 0)
    fb.take(0, 0)
    for turn_of in range(2):
        fc.launch(0, turn_of)
        fd.launch(0, turn_of)
    pass_z(0)
    pass_x(1)
    own.wait_recv()
    use(twin_shard, 0)
    use(twin_shard, 1)
    pass_z(1)
    fa.take(0, 1)
    fb.take(0, 1)
    use(twin_shard, 2)
    use(twin_shard, 3)
    fa.take(1, 0)
    fb.take(1, 0)
    use(side, here)
    pass_z(2)
    fc.take(0, 0)
    fd.take(0, 0)
    fa.take(1, 1)
    fb.take(1, 1)
    pass_z(3)
    use(side, there_x)
    use(side, there_z)
    fa.take(2, 0)
    fb.take(2, 0)
    fc.take(0, 1)
    fd.take(0, 1)
    use(side, there)
    for copy in from_twin[:2]:
        copy.wait_recv()
    use(twin_side, here)
    fc.take(1, 0)
    fd.take(1, 0)
    fa.take(2, 1)
    fb.take(2, 1)
    for copy in from_twin[2:]:
        copy.wait_recv()
    use(twin_side, there_x)
    use(twin_side, there_z)
    fc.take(1, 1)
    fd.take(1, 1)
    use(twin_side, there)
    fc.take(2, 0)
    fd.take(2, 0)
    for h in range(heads):
        cols = slice(h * HEAD_DIM, (h + 1) * HEAD_DIM)
        rot_ref[:, cols] = turn(proj[:, cols], 1.0).astype(jnp.bfloat16)
    fa.finish(slice(0, quarter))
    fb.finish(slice(quarter, 2 * quarter))
    fc.take(2, 1)
    fd.take(2, 1)
    fc.finish(slice(2 * quarter, 3 * quarter))
    fd.finish(slice(3 * quarter, block))

    for group in range(4):
        group_copy(group // 2, group % 2).wait_send()
    for copy in started:
        copy.wait_send()


def fused_body(tokens, quant_weight, block_scales, key_grad):
    row_count, model = tokens.shape
    shard_rows, width = quant_weight.shape
    block = model // (lax.axis_size("rep") * lax.axis_size("fsdp"))
    bf16, f32 = jnp.bfloat16, jnp.float32
    vmem = pl.BlockSpec(memory_space=pltpu.VMEM)
    hbm = pl.BlockSpec(memory_space=pltpu.HBM)
    flows = [
        pltpu.VMEM((2,) * (4 - level) + (block // 4, width), bf16)
        for level in range(5)
        for _ in range(4)
    ]
    results = pl.pallas_call(
        fused_kernel,
        out_shape=[
            pltpu.VMEM((row_count, width), bf16),
            pltpu.VMEM((row_count, model), bf16),
            pltpu.VMEM((block, width), bf16),
        ],
        in_specs=[hbm, hbm, vmem, hbm],
        out_specs=[vmem] * 3,
        scratch_shapes=[
            pltpu.VMEM((row_count, model), bf16),
            pltpu.VMEM((shard_rows, width), bf16),
            pltpu.VMEM((row_count, width), bf16),
            pltpu.VMEM((4, 8, shard_rows // 8, width), bf16),
            pltpu.VMEM((2, 2, row_count, 4 * block), bf16),
            pltpu.VMEM((2, row_count, width), bf16),
            pltpu.VMEM((row_count, width), f32),
            pltpu.VMEM((row_count, HEAD_DIM), f32),
            pltpu.VMEM((row_count, HEAD_DIM), f32),
            *flows,
            pltpu.SemaphoreType.DMA((3,)),
            pltpu.SemaphoreType.DMA((8,)),
            pltpu.SemaphoreType.DMA((2,)),
            pltpu.SemaphoreType.DMA((17,)),
            pltpu.SemaphoreType.DMA((17,)),
            pltpu.SemaphoreType.DMA((32,)),
            pltpu.SemaphoreType.DMA((32,)),
        ],
        compiler_params=pltpu.CompilerParams(
            collective_id=0, has_side_effects=True, vmem_limit_bytes=56 * 1024 * 1024
        ),
    )(tokens, quant_weight, block_scales, key_grad)
    return pl.pallas_call(
        place_kernel,
        out_shape=[jax.ShapeDtypeStruct(value.shape, value.dtype) for value in results],
        in_specs=[vmem] * 3,
        out_specs=[hbm] * 3,
        scratch_shapes=[pltpu.SemaphoreType.DMA((3,))],
    )(*results)


def place_kernel(rot_in, tg_in, wg_in, rot_out, tg_out, wg_out, sems):
    pairs = ((tg_in, tg_out), (rot_in, rot_out), (wg_in, wg_out))
    copies = [
        pltpu.make_async_copy(source, target, sems.at[i])
        for i, (source, target) in enumerate(pairs)
    ]
    for copy in copies:
        copy.start()
    for copy in copies:
        copy.wait()


def solution(mesh):
    paired = mesh.shape["rep"] == 8 and mesh.shape["fsdp"] == 4
    return jax.shard_map(
        fused_body if paired else body,
        mesh=mesh,
        in_specs=(P(("rep", "fsdp"), None), P("fsdp", None), P("fsdp"), P(("rep", "fsdp"), None)),
        out_specs=(P(("rep", "fsdp"), None), P(("rep", "fsdp"), None), P(("rep", "fsdp"), None)),
        check_vma=False,
    )
```

```python
import math

import jax
import jax.numpy as jnp
from jax import lax
from jax.experimental import pallas as pl
from jax.experimental.pallas import tpu as pltpu
from jax.sharding import PartitionSpec as P

HEAD_DIM = 128


rope_base = 10000.0


def dequantize(quant_weight, block_scales):
    rows_per_block = quant_weight.shape[0] // block_scales.shape[0]
    scaled = quant_weight.astype(jnp.float32).reshape(
        block_scales.shape[0], rows_per_block, quant_weight.shape[1]
    )
    scaled = scaled * block_scales.astype(jnp.float32)[:, None, None]
    return scaled.reshape(quant_weight.shape).astype(jnp.bfloat16)


def rotary(projected, positions, direction):
    half_size = HEAD_DIM // 2
    steps = jnp.arange(half_size, dtype=jnp.int32).astype(jnp.float32)
    frequency = jnp.exp(steps * (-2.0 * math.log(rope_base) / HEAD_DIM))
    angles = positions[:, None] * frequency[None, :]
    cosine = jnp.cos(angles)[:, None, :]
    sine_part = direction * jnp.sin(angles)[:, None, :]
    halves = projected.reshape(projected.shape[0], -1, 2, half_size)
    leading = halves[:, :, 0]
    trailing = halves[:, :, 1]
    turned = jnp.stack(
        [leading * cosine - trailing * sine_part, trailing * cosine + leading * sine_part], axis=2
    )
    return turned.reshape(projected.shape)


def partial_rows(source, proj_grad):
    return lax.dot_general(
        source, proj_grad, (((0,), (0,)), ((), ())), preferred_element_type=jnp.float32
    )


def body(tokens, quant_weight, block_scales, key_grad):
    row_count = tokens.shape[0]
    all_codes, all_scales = (
        lax.all_gather(quant_weight, "fsdp", axis=0, tiled=True),
        lax.all_gather(block_scales, "fsdp", axis=0, tiled=True),
    )
    weight = dequantize(all_codes, all_scales)
    positions = (
        lax.axis_index("fsdp") * row_count + jnp.arange(row_count, dtype=jnp.int32)
    ).astype(jnp.float32)
    projected = jnp.dot(tokens, weight, preferred_element_type=jnp.float32)
    rotated = rotary(projected, positions, 1.0).astype(jnp.bfloat16)
    proj_grad = rotary(key_grad.astype(jnp.float32), positions, -1.0).astype(jnp.bfloat16)
    token_grad = lax.dot_general(
        proj_grad, weight, (((1,), (1,)), ((), ())), preferred_element_type=jnp.float32
    ).astype(jnp.bfloat16)
    total_rows = weight.shape[0]
    fsdp_size = lax.axis_size("fsdp")
    rep_size = lax.axis_size("rep")
    share = total_rows // (fsdp_size * rep_size)
    reordered = (
        tokens.reshape(row_count, rep_size, fsdp_size, share)
        .transpose(0, 2, 1, 3)
        .reshape(row_count, total_rows)
    )
    group_sum = lax.psum_scatter(
        partial_rows(reordered, proj_grad).astype(jnp.bfloat16),
        "fsdp",
        scatter_dimension=0,
        tiled=True,
    ).astype(jnp.float32)
    summed = lax.psum_scatter(group_sum, "rep", scatter_dimension=0, tiled=True)
    weight_grad = (summed * (1.0 / math.sqrt(row_count * fsdp_size * rep_size))).astype(
        jnp.bfloat16
    )
    return (rotated, token_grad, weight_grad)


MESH = pl.DeviceIdType.MESH


def fused_kernel(
    tok_hbm, quant_hbm, scale_ref, kg_hbm,
    rot_ref, tg_ref, wg_ref,
    tok_ref, quant_ref, kg_ref, kg_twin,
    wbuf, tok_twin, pg, proj, cos_t, sin_t,
    sa, sb, sc, sd, a1, b1, c1, d1, a2, b2, c2, d2, a3, b3, c3, d3, a4, b4, c4, d4,
    load_sem, tok_sem, pg_sem, w_send, w_recv, rs_send, rs_recv,
):
    rep, fsdp = lax.axis_index("rep"), lax.axis_index("fsdp")
    x, z0, z1 = rep % 2, (rep // 2) % 2, rep // 4
    y, c = fsdp // 2, fsdp % 2
    twin = (rep, fsdp + 1 - 2 * c)
    over_y = (rep, fsdp + 2 - 4 * y)
    over_x = (rep + 1 - 2 * x, fsdp)
    over_z0 = (rep + 2 - 4 * z0, fsdp)
    over_z1 = (rep + 4 - 8 * z1, fsdp)
    row_count, width = kg_ref.shape
    shard_rows = quant_ref.shape[0]
    piece = shard_rows // 4
    part = shard_rows // 8
    block = wg_ref.shape[0]
    here = 2 * x + z0

    load_quant = pltpu.make_async_copy(quant_hbm, quant_ref, load_sem.at[0])
    load_quant.start()
    load_kg = pltpu.make_async_copy(kg_hbm, kg_ref, load_sem.at[1])
    load_kg.start()
    load_tok = pltpu.make_async_copy(tok_hbm, tok_ref, load_sem.at[2])
    load_tok.start()

    barrier = pltpu.get_barrier_semaphore()
    for other in (twin, over_y, over_x, over_z0, over_z1):
        pl.semaphore_signal(barrier, inc=1, device_id=other, device_id_type=MESH)

    def dequant(i):
        rows = pl.ds(pl.multiple_of(i * part, part), part)
        n_blocks = scale_ref.shape[0]
        per_block = shard_rows // n_blocks
        owner = (i * part + lax.broadcasted_iota(jnp.int32, (part, n_blocks), 0)) // per_block
        lane = lax.broadcasted_iota(jnp.int32, (part, n_blocks), 1)
        picked = jnp.where(owner == lane, scale_ref[...].astype(jnp.float32).reshape(1, n_blocks), 0.0)
        column = jnp.sum(picked, axis=1, keepdims=True)
        wbuf[fsdp, i] = (quant_ref[rows, :].astype(jnp.float32) * column).astype(jnp.bfloat16)

    load_quant.wait()
    dequant(2 * here)
    dequant(2 * here + 1)
    pl.semaphore_wait(barrier, 5)

    started = []

    def send(src, dst, send_sem, recv_sem, to):
        copy = pltpu.make_async_remote_copy(
            src_ref=src, dst_ref=dst, send_sem=send_sem, recv_sem=recv_sem,
            device_id=to, device_id_type=MESH,
        )
        copy.start()
        started.append(copy)
        return copy

    def send_w(shard, i, slot, to):
        return send(
            wbuf.at[shard, i], wbuf.at[shard, i], w_send.at[slot], w_recv.at[slot], to
        )

    from_y = [send_w(fsdp, 2 * here + q, q, over_y) for q in range(2)]

    def send_tokens(bx, by):
        group = 2 * bx + by
        for k in range(4):
            col = pl.multiple_of(((k % 2 * 8 + k // 2 * 4 + group) * 2 + 1 - c) * block, block)
            pltpu.make_async_remote_copy(
                src_ref=tok_ref.at[:, pl.ds(col, block)],
                dst_ref=tok_twin.at[bx, by, :, pl.ds(k * block, block)],
                send_sem=tok_sem.at[group], recv_sem=tok_sem.at[4 + group],
                device_id=twin, device_id_type=MESH,
            ).start()

    def group_copy(bx, by):
        group = 2 * bx + by
        return pltpu.make_async_remote_copy(
            src_ref=tok_twin.at[bx, by], dst_ref=tok_twin.at[bx, by],
            send_sem=tok_sem.at[group], recv_sem=tok_sem.at[4 + group],
            device_id=twin, device_id_type=MESH,
        )

    load_kg.wait()
    kg_copy = send(kg_ref, kg_twin, pg_sem.at[0], pg_sem.at[1], twin)
    load_tok.wait()
    send_tokens(1 - x, 1 - y)
    send_tokens(1 - x, y)
    send_tokens(x, 1 - y)
    send_tokens(x, y)

    half = HEAD_DIM // 2
    low_rows = 8
    high_rows = row_count // low_rows

    def angles(rows, first, step):
        shape = (rows, HEAD_DIM)
        steps = (lax.broadcasted_iota(jnp.int32, shape, 1) % half).astype(jnp.float32)
        frequency = jnp.exp(steps * (-2.0 * math.log(rope_base) / HEAD_DIM))
        place = first + step * lax.broadcasted_iota(jnp.int32, shape, 0)
        return place.astype(jnp.float32) * frequency

    low = angles(low_rows, 0, 1)
    cos_low, sin_low = jnp.cos(low), jnp.sin(low)
    leading = lax.broadcasted_iota(jnp.int32, (low_rows, HEAD_DIM), 1) < half
    heads = width // HEAD_DIM

    def turn(value, whose, direction):
        flipped = pltpu.roll(value, half, 1) * (direction * sin_t[whose])
        return value * cos_t[whose] + flipped

    def make_pg(whose, owner, source):
        high = angles(high_rows, owner * row_count, low_rows)
        cos_high, sin_high = jnp.cos(high), jnp.sin(high)
        for i in range(high_rows):
            rows = slice(i * low_rows, (i + 1) * low_rows)
            ch, sh = cos_high[i : i + 1], sin_high[i : i + 1]
            cos_t[whose, rows, :] = ch * cos_low - sh * sin_low
            sine = sh * cos_low + ch * sin_low
            sin_t[whose, rows, :] = jnp.where(leading, -sine, sine)
        for h in range(heads):
            cols = slice(h * HEAD_DIM, (h + 1) * HEAD_DIM)
            value = source[:, cols].astype(jnp.float32)
            pg[whose, :, cols] = turn(value, whose, -1.0).astype(jnp.bfloat16)

    make_pg(0, fsdp, kg_ref)
    kg_copy.wait_recv()
    make_pg(1, fsdp + 1 - 2 * c, kg_twin)

    quarter = block // 4

    def blocks(bx, by):
        group_copy(bx, by).wait_recv()
        own_columns = [
            tok_ref[:, pl.ds(pl.multiple_of(((k % 2 * 8 + k // 2 * 4 + 2 * bx + by) * 2 + c) * block, block), block)]
            for k in range(4)
        ]
        left = jnp.concatenate(
            [jnp.concatenate(own_columns, axis=1), tok_twin[bx, by]], axis=0
        )
        right = pg[...].reshape(2 * row_count, width)
        total = lax.dot_general(
            left, right, (((0,), (0,)), ((), ())), preferred_element_type=jnp.float32
        ).astype(jnp.bfloat16).reshape(2, 2, 4, quarter, width)
        sa[bx, by] = total[:, :, 0]
        sb[by, bx] = total[:, :, 1]
        for bz0 in range(2):
            sc[bx, bz0, by] = total[bz0, :, 2]
            sd[by, bz0, bx] = total[bz0, :, 3]

    class Flow:
        def __init__(self, index, bits, others, bufs):
            self.index, self.bits, self.others, self.bufs = index, bits, others, bufs
            self.copies = {}

        def launch(self, stage, turn_of):
            bits, bufs = self.bits, self.bufs
            slot = self.index * 8 + stage * 2 + turn_of
            sems = (rs_send.at[slot], rs_recv.at[slot], self.others[stage])
            lead = 1 - bits[stage]
            if stage == 3:
                src, dst = bufs[3].at[lead], bufs[4]
            else:
                sub = 1 - bits[stage + 1] if turn_of == 0 else bits[stage + 1]
                src, dst = bufs[stage].at[lead, sub], bufs[stage + 1].at[sub]
            self.copies[stage, turn_of] = send(src, dst, *sems)

        def take(self, stage, turn_of):
            bits, bufs = self.bits, self.bufs
            self.copies[stage, turn_of].wait_recv()
            sub = 1 - bits[stage + 1] if turn_of == 0 else bits[stage + 1]
            mine = bufs[stage][bits[stage], sub].astype(jnp.float32)
            bufs[stage + 1][sub] = (
                bufs[stage + 1][sub].astype(jnp.float32) + mine
            ).astype(jnp.bfloat16)
            if turn_of == 0:
                self.launch(stage + 1, 0)
                if stage + 1 < 3:
                    self.launch(stage + 1, 1)

        def finish(self, rows):
            bits, bufs = self.bits, self.bufs
            self.copies[3, 0].wait_recv()
            total = bufs[4][...].astype(jnp.float32) + bufs[3][bits[3]].astype(jnp.float32)
            count = row_count * lax.axis_size("rep") * lax.axis_size("fsdp")
            wg_ref[rows, :] = (total * (1.0 / math.sqrt(count))).astype(jnp.bfloat16)

    x_first = ((x, y, z0, z1), (over_x, over_y, over_z0, over_z1))
    y_first = ((y, x, z0, z1), (over_y, over_x, over_z0, over_z1))
    fa = Flow(0, *x_first, (sa, a1, a2, a3, a4))
    fb = Flow(1, *y_first, (sb, b1, b2, b3, b4))
    x_then_z = ((x, z0, y, z1), (over_x, over_z0, over_y, over_z1))
    y_then_z = ((y, z0, x, z1), (over_y, over_z0, over_x, over_z1))
    fc = Flow(2, *x_then_z, (sc, c1, c2, c3, c4))
    fd = Flow(3, *y_then_z, (sd, d1, d2, d3, d4))

    def use(shard, at):
        col = pl.multiple_of(shard * shard_rows + at * piece, piece)
        cols = pl.ds(col, piece)
        w = wbuf[shard, pl.ds(2 * at, 2)].reshape(piece, width)
        tg_ref[:, cols] = lax.dot_general(
            pg[0], w, (((1,), (1,)), ((), ())), preferred_element_type=jnp.float32
        ).astype(jnp.bfloat16)
        proj[...] += jnp.dot(tok_ref[:, cols], w, preferred_element_type=jnp.float32)

    def use_all(shard):
        def one(i, carry):
            use(shard, i)
            return carry

        lax.fori_loop(0, 4, one, 0)

    side = fsdp + 2 - 4 * y
    twin_shard = fsdp + 1 - 2 * c
    twin_side = side + 1 - 2 * c
    there_x, there_z, there = 2 * (1 - x) + z0, 2 * x + 1 - z0, 3 - here
    from_x, from_z, from_twin = [], [], []

    def pass_y(q):
        i = 2 * here + q
        from_y[q].wait_recv()
        from_x.append(send_w(side, i, 2 + q, over_x))
        from_z.append(send_w(side, i, 4 + q, over_z0))
        from_twin.append(send_w(side, i, 8 + q, twin))

    def pass_x(q):
        i = 2 * there_x + q
        from_x[q].wait_recv()
        from_z.append(send_w(side, i, 6 + q, over_z0))
        from_twin.append(send_w(side, i, 10 + q, twin))

    def pass_z(q):
        i = 2 * (there_z if q < 2 else there) + q % 2
        from_z[q].wait_recv()
        from_twin.append(send_w(side, i, 12 + q, twin))

    proj[...] = jnp.zeros_like(proj)
    blocks(1 - x, 1 - y)
    fa.launch(0, 0)
    fb.launch(0, 0)
    pass_y(0)
    blocks(1 - x, y)
    blocks(x, 1 - y)
    fa.launch(0, 1)
    fb.launch(0, 1)
    pass_y(1)
    blocks(x, y)
    def dequant_other(i, carry):
        other = (2 * here + 2 + i) % 8
        dequant(other)
        return carry

    lax.fori_loop(0, 6, dequant_other, 0)
    own = send(wbuf.at[fsdp], wbuf.at[fsdp], w_send.at[16], w_recv.at[16], twin)
    use_all(fsdp)
    pass_x(0)
    fa.take(0, 0)
    fb.take(0, 0)
    for turn_of in range(2):
        fc.launch(0, turn_of)
        fd.launch(0, turn_of)
    pass_z(0)
    pass_x(1)
    own.wait_recv()
    use(twin_shard, 0)
    use(twin_shard, 1)
    pass_z(1)
    fa.take(0, 1)
    fb.take(0, 1)
    use(twin_shard, 2)
    use(twin_shard, 3)
    fa.take(1, 0)
    fb.take(1, 0)
    use(side, here)
    pass_z(2)
    fc.take(0, 0)
    fd.take(0, 0)
    fa.take(1, 1)
    fb.take(1, 1)
    pass_z(3)
    use(side, there_x)
    use(side, there_z)
    fa.take(2, 0)
    fb.take(2, 0)
    fc.take(0, 1)
    fd.take(0, 1)
    use(side, there)
    for copy in from_twin[:2]:
        copy.wait_recv()
    use(twin_side, here)
    fc.take(1, 0)
    fd.take(1, 0)
    fa.take(2, 1)
    fb.take(2, 1)
    for copy in from_twin[2:]:
        copy.wait_recv()
    use(twin_side, there_x)
    use(twin_side, there_z)
    fc.take(1, 1)
    fd.take(1, 1)
    use(twin_side, there)
    fc.take(2, 0)
    fd.take(2, 0)
    for h in range(heads):
        cols = slice(h * HEAD_DIM, (h + 1) * HEAD_DIM)
        rot_ref[:, cols] = turn(proj[:, cols], 0, 1.0).astype(jnp.bfloat16)
    fa.finish(slice(0, quarter))
    fb.finish(slice(quarter, 2 * quarter))
    fc.take(2, 1)
    fd.take(2, 1)
    fc.finish(slice(2 * quarter, 3 * quarter))
    fd.finish(slice(3 * quarter, block))

    for group in range(4):
        group_copy(group // 2, group % 2).wait_send()
    for copy in started:
        copy.wait_send()


def fused_body(tokens, quant_weight, block_scales, key_grad):
    row_count, model = tokens.shape
    shard_rows, width = quant_weight.shape
    block = model // (lax.axis_size("rep") * lax.axis_size("fsdp"))
    bf16, f32 = jnp.bfloat16, jnp.float32
    vmem = pl.BlockSpec(memory_space=pltpu.VMEM)
    hbm = pl.BlockSpec(memory_space=pltpu.HBM)
    flows = [
        pltpu.VMEM((2,) * (4 - level) + (block // 4, width), bf16)
        for level in range(5)
        for _ in range(4)
    ]
    results = pl.pallas_call(
        fused_kernel,
        out_shape=[
            pltpu.VMEM((row_count, width), bf16),
            pltpu.VMEM((row_count, model), bf16),
            pltpu.VMEM((block, width), bf16),
        ],
        in_specs=[hbm, hbm, vmem, hbm],
        out_specs=[vmem] * 3,
        scratch_shapes=[
            pltpu.VMEM((row_count, model), bf16),
            pltpu.VMEM((shard_rows, width), bf16),
            pltpu.VMEM((row_count, width), bf16),
            pltpu.VMEM((row_count, width), bf16),
            pltpu.VMEM((4, 8, shard_rows // 8, width), bf16),
            pltpu.VMEM((2, 2, row_count, 4 * block), bf16),
            pltpu.VMEM((2, row_count, width), bf16),
            pltpu.VMEM((row_count, width), f32),
            pltpu.VMEM((2, row_count, HEAD_DIM), f32),
            pltpu.VMEM((2, row_count, HEAD_DIM), f32),
            *flows,
            pltpu.SemaphoreType.DMA((3,)),
            pltpu.SemaphoreType.DMA((8,)),
            pltpu.SemaphoreType.DMA((2,)),
            pltpu.SemaphoreType.DMA((17,)),
            pltpu.SemaphoreType.DMA((17,)),
            pltpu.SemaphoreType.DMA((32,)),
            pltpu.SemaphoreType.DMA((32,)),
        ],
        compiler_params=pltpu.CompilerParams(
            collective_id=0, has_side_effects=True, vmem_limit_bytes=56 * 1024 * 1024
        ),
    )(tokens, quant_weight, block_scales, key_grad)
    return pl.pallas_call(
        place_kernel,
        out_shape=[jax.ShapeDtypeStruct(value.shape, value.dtype) for value in results],
        in_specs=[vmem] * 3,
        out_specs=[hbm] * 3,
        scratch_shapes=[pltpu.SemaphoreType.DMA((3,))],
        compiler_params=pltpu.CompilerParams(vmem_limit_bytes=4 * 1024 * 1024),
    )(*results)


def place_kernel(rot_in, tg_in, wg_in, rot_out, tg_out, wg_out, sems):
    pairs = ((tg_in, tg_out), (rot_in, rot_out), (wg_in, wg_out))
    copies = [
        pltpu.make_async_copy(source, target, sems.at[i])
        for i, (source, target) in enumerate(pairs)
    ]
    for copy in copies:
        copy.start()
    for copy in copies:
        copy.wait()


def solution(mesh):
    paired = mesh.shape["rep"] == 8 and mesh.shape["fsdp"] == 4
    return jax.shard_map(
        fused_body if paired else body,
        mesh=mesh,
        in_specs=(P(("rep", "fsdp"), None), P("fsdp", None), P("fsdp"), P(("rep", "fsdp"), None)),
        out_specs=(P(("rep", "fsdp"), None), P(("rep", "fsdp"), None), P(("rep", "fsdp"), None)),
        check_vma=False,
    )
```

```python
import math

import jax
import jax.numpy as jnp
from jax import lax
from jax.experimental import pallas as pl
from jax.experimental.pallas import tpu as pltpu
from jax.sharding import PartitionSpec as P

HEAD_DIM = 128


rope_base = 10000.0


def dequantize(quant_weight, block_scales):
    rows_per_block = quant_weight.shape[0] // block_scales.shape[0]
    scaled = quant_weight.astype(jnp.float32).reshape(
        block_scales.shape[0], rows_per_block, quant_weight.shape[1]
    )
    scaled = scaled * block_scales.astype(jnp.float32)[:, None, None]
    return scaled.reshape(quant_weight.shape).astype(jnp.bfloat16)


def rotary(projected, positions, direction):
    half_size = HEAD_DIM // 2
    steps = jnp.arange(half_size, dtype=jnp.int32).astype(jnp.float32)
    frequency = jnp.exp(steps * (-2.0 * math.log(rope_base) / HEAD_DIM))
    angles = positions[:, None] * frequency[None, :]
    cosine = jnp.cos(angles)[:, None, :]
    sine_part = direction * jnp.sin(angles)[:, None, :]
    halves = projected.reshape(projected.shape[0], -1, 2, half_size)
    leading = halves[:, :, 0]
    trailing = halves[:, :, 1]
    turned = jnp.stack(
        [leading * cosine - trailing * sine_part, trailing * cosine + leading * sine_part], axis=2
    )
    return turned.reshape(projected.shape)


def partial_rows(source, proj_grad):
    return lax.dot_general(
        source, proj_grad, (((0,), (0,)), ((), ())), preferred_element_type=jnp.float32
    )


def body(tokens, quant_weight, block_scales, key_grad):
    row_count = tokens.shape[0]
    all_codes, all_scales = (
        lax.all_gather(quant_weight, "fsdp", axis=0, tiled=True),
        lax.all_gather(block_scales, "fsdp", axis=0, tiled=True),
    )
    weight = dequantize(all_codes, all_scales)
    positions = (
        lax.axis_index("fsdp") * row_count + jnp.arange(row_count, dtype=jnp.int32)
    ).astype(jnp.float32)
    projected = jnp.dot(tokens, weight, preferred_element_type=jnp.float32)
    rotated = rotary(projected, positions, 1.0).astype(jnp.bfloat16)
    proj_grad = rotary(key_grad.astype(jnp.float32), positions, -1.0).astype(jnp.bfloat16)
    token_grad = lax.dot_general(
        proj_grad, weight, (((1,), (1,)), ((), ())), preferred_element_type=jnp.float32
    ).astype(jnp.bfloat16)
    total_rows = weight.shape[0]
    fsdp_size = lax.axis_size("fsdp")
    rep_size = lax.axis_size("rep")
    share = total_rows // (fsdp_size * rep_size)
    reordered = (
        tokens.reshape(row_count, rep_size, fsdp_size, share)
        .transpose(0, 2, 1, 3)
        .reshape(row_count, total_rows)
    )
    group_sum = lax.psum_scatter(
        partial_rows(reordered, proj_grad).astype(jnp.bfloat16),
        "fsdp",
        scatter_dimension=0,
        tiled=True,
    ).astype(jnp.float32)
    summed = lax.psum_scatter(group_sum, "rep", scatter_dimension=0, tiled=True)
    weight_grad = (summed * (1.0 / math.sqrt(row_count * fsdp_size * rep_size))).astype(
        jnp.bfloat16
    )
    return (rotated, token_grad, weight_grad)


MESH = pl.DeviceIdType.MESH


def fused_kernel(
    tok_hbm, quant_hbm, scale_ref, kg_hbm,
    rot_ref, tg_ref, wg_ref,
    tok_ref, quant_ref, kg_ref, kg_twin,
    wbuf, tok_twin, pg, proj, cos_t, sin_t,
    sa, sb, sc, sd, a1, b1, c1, d1, a2, b2, c2, d2, a3, b3, c3, d3, a4, b4, c4, d4,
    load_sem, tok_sem, pg_sem, w_send, w_recv, rs_send, rs_recv,
):
    rep, fsdp = lax.axis_index("rep"), lax.axis_index("fsdp")
    x, z0, z1 = rep % 2, (rep // 2) % 2, rep // 4
    y, c = fsdp // 2, fsdp % 2
    twin = (rep, fsdp + 1 - 2 * c)
    over_y = (rep, fsdp + 2 - 4 * y)
    over_x = (rep + 1 - 2 * x, fsdp)
    over_z0 = (rep + 2 - 4 * z0, fsdp)
    over_z1 = (rep + 4 - 8 * z1, fsdp)
    row_count, width = kg_ref.shape
    shard_rows = quant_ref.shape[0]
    piece = shard_rows // 4
    part = shard_rows // 8
    block = wg_ref.shape[0]
    here = 2 * x + z0

    load_quant = pltpu.make_async_copy(quant_hbm, quant_ref, load_sem.at[0])
    load_quant.start()
    load_kg = pltpu.make_async_copy(kg_hbm, kg_ref, load_sem.at[1])
    load_kg.start()
    load_tok = pltpu.make_async_copy(tok_hbm, tok_ref, load_sem.at[2])
    load_tok.start()

    barrier = pltpu.get_barrier_semaphore()
    for other in (twin, over_y, over_x, over_z0, over_z1):
        pl.semaphore_signal(barrier, inc=1, device_id=other, device_id_type=MESH)

    def dequant(i):
        rows = pl.ds(pl.multiple_of(i * part, part), part)
        n_blocks = scale_ref.shape[0]
        per_block = shard_rows // n_blocks
        owner = (i * part + lax.broadcasted_iota(jnp.int32, (part, n_blocks), 0)) // per_block
        lane = lax.broadcasted_iota(jnp.int32, (part, n_blocks), 1)
        picked = jnp.where(owner == lane, scale_ref[...].astype(jnp.float32).reshape(1, n_blocks), 0.0)
        column = jnp.sum(picked, axis=1, keepdims=True)
        wbuf[fsdp, i] = (quant_ref[rows, :].astype(jnp.float32) * column).astype(jnp.bfloat16)

    load_quant.wait()
    dequant(2 * here)
    dequant(2 * here + 1)
    pl.semaphore_wait(barrier, 5)

    started = []

    def send(src, dst, send_sem, recv_sem, to):
        copy = pltpu.make_async_remote_copy(
            src_ref=src, dst_ref=dst, send_sem=send_sem, recv_sem=recv_sem,
            device_id=to, device_id_type=MESH,
        )
        copy.start()
        started.append(copy)
        return copy

    def send_w(shard, i, slot, to):
        return send(
            wbuf.at[shard, i], wbuf.at[shard, i], w_send.at[slot], w_recv.at[slot], to
        )

    from_y = [send_w(fsdp, 2 * here + q, q, over_y) for q in range(2)]

    def send_tokens(bx, by):
        group = 2 * bx + by
        for k in range(4):
            col = pl.multiple_of(((k % 2 * 8 + k // 2 * 4 + group) * 2 + 1 - c) * block, block)
            pltpu.make_async_remote_copy(
                src_ref=tok_ref.at[:, pl.ds(col, block)],
                dst_ref=tok_twin.at[bx, by, :, pl.ds(k * block, block)],
                send_sem=tok_sem.at[group], recv_sem=tok_sem.at[4 + group],
                device_id=twin, device_id_type=MESH,
            ).start()

    def group_copy(bx, by):
        group = 2 * bx + by
        return pltpu.make_async_remote_copy(
            src_ref=tok_twin.at[bx, by], dst_ref=tok_twin.at[bx, by],
            send_sem=tok_sem.at[group], recv_sem=tok_sem.at[4 + group],
            device_id=twin, device_id_type=MESH,
        )

    load_kg.wait()
    kg_copy = send(kg_ref, kg_twin, pg_sem.at[0], pg_sem.at[1], twin)
    load_tok.wait()
    send_tokens(1 - x, 1 - y)
    send_tokens(1 - x, y)
    send_tokens(x, 1 - y)
    send_tokens(x, y)

    half = HEAD_DIM // 2
    low_rows = 8
    high_rows = row_count // low_rows

    def angles(rows, first, step):
        shape = (rows, HEAD_DIM)
        steps = (lax.broadcasted_iota(jnp.int32, shape, 1) % half).astype(jnp.float32)
        frequency = jnp.exp(steps * (-2.0 * math.log(rope_base) / HEAD_DIM))
        place = first + step * lax.broadcasted_iota(jnp.int32, shape, 0)
        return place.astype(jnp.float32) * frequency

    low = angles(low_rows, 0, 1)
    cos_low, sin_low = jnp.cos(low), jnp.sin(low)
    leading = lax.broadcasted_iota(jnp.int32, (low_rows, HEAD_DIM), 1) < half
    heads = width // HEAD_DIM

    def turn(value, whose, direction):
        flipped = pltpu.roll(value, half, 1) * (direction * sin_t[whose])
        return value * cos_t[whose] + flipped

    def make_pg(whose, owner, source):
        high = angles(high_rows, owner * row_count, low_rows)
        cos_high, sin_high = jnp.cos(high), jnp.sin(high)
        for i in range(high_rows):
            rows = slice(i * low_rows, (i + 1) * low_rows)
            ch, sh = cos_high[i : i + 1], sin_high[i : i + 1]
            cos_t[whose, rows, :] = ch * cos_low - sh * sin_low
            sine = sh * cos_low + ch * sin_low
            sin_t[whose, rows, :] = jnp.where(leading, -sine, sine)
        for h in range(heads):
            cols = slice(h * HEAD_DIM, (h + 1) * HEAD_DIM)
            value = source[:, cols].astype(jnp.float32)
            pg[whose, :, cols] = turn(value, whose, -1.0).astype(jnp.bfloat16)

    make_pg(0, fsdp, kg_ref)
    kg_copy.wait_recv()
    make_pg(1, fsdp + 1 - 2 * c, kg_twin)

    quarter = block // 4

    def blocks(bx, by):
        group_copy(bx, by).wait_recv()
        own_columns = [
            tok_ref[:, pl.ds(pl.multiple_of(((k % 2 * 8 + k // 2 * 4 + 2 * bx + by) * 2 + c) * block, block), block)]
            for k in range(4)
        ]
        left = jnp.concatenate(
            [jnp.concatenate(own_columns, axis=1), tok_twin[bx, by]], axis=0
        )
        right = pg[...].reshape(2 * row_count, width)
        total = lax.dot_general(
            left, right, (((0,), (0,)), ((), ())), preferred_element_type=jnp.float32
        ).astype(jnp.bfloat16).reshape(2, 2, 4, quarter, width)
        sa[bx, by] = total[:, :, 0]
        sb[by, bx] = total[:, :, 1]
        for bz0 in range(2):
            sc[bx, bz0, by] = total[bz0, :, 2]
            sd[by, bz0, bx] = total[bz0, :, 3]

    class Flow:
        def __init__(self, index, bits, others, bufs):
            self.index, self.bits, self.others, self.bufs = index, bits, others, bufs
            self.copies = {}

        def launch(self, stage, turn_of):
            bits, bufs = self.bits, self.bufs
            slot = self.index * 8 + stage * 2 + turn_of
            sems = (rs_send.at[slot], rs_recv.at[slot], self.others[stage])
            lead = 1 - bits[stage]
            if stage == 3:
                src, dst = bufs[3].at[lead], bufs[4]
            else:
                sub = 1 - bits[stage + 1] if turn_of == 0 else bits[stage + 1]
                src, dst = bufs[stage].at[lead, sub], bufs[stage + 1].at[sub]
            self.copies[stage, turn_of] = send(src, dst, *sems)

        def take(self, stage, turn_of):
            bits, bufs = self.bits, self.bufs
            self.copies[stage, turn_of].wait_recv()
            sub = 1 - bits[stage + 1] if turn_of == 0 else bits[stage + 1]
            mine = bufs[stage][bits[stage], sub].astype(jnp.float32)
            bufs[stage + 1][sub] = (
                bufs[stage + 1][sub].astype(jnp.float32) + mine
            ).astype(jnp.bfloat16)
            if turn_of == 0:
                self.launch(stage + 1, 0)
                if stage + 1 < 3:
                    self.launch(stage + 1, 1)

        def finish(self, rows):
            bits, bufs = self.bits, self.bufs
            self.copies[3, 0].wait_recv()
            total = bufs[4][...].astype(jnp.float32) + bufs[3][bits[3]].astype(jnp.float32)
            count = row_count * lax.axis_size("rep") * lax.axis_size("fsdp")
            wg_ref[rows, :] = (total * (1.0 / math.sqrt(count))).astype(jnp.bfloat16)

    x_first = ((x, y, z0, z1), (over_x, over_y, over_z0, over_z1))
    y_first = ((y, x, z0, z1), (over_y, over_x, over_z0, over_z1))
    fa = Flow(0, *x_first, (sa, a1, a2, a3, a4))
    fb = Flow(1, *y_first, (sb, b1, b2, b3, b4))
    x_then_z = ((x, z0, y, z1), (over_x, over_z0, over_y, over_z1))
    y_then_z = ((y, z0, x, z1), (over_y, over_z0, over_x, over_z1))
    fc = Flow(2, *x_then_z, (sc, c1, c2, c3, c4))
    fd = Flow(3, *y_then_z, (sd, d1, d2, d3, d4))

    def use(shard, at):
        col = pl.multiple_of(shard * shard_rows + at * piece, piece)
        cols = pl.ds(col, piece)
        w = wbuf[shard, pl.ds(2 * at, 2)].reshape(piece, width)
        tg_ref[:, cols] = lax.dot_general(
            pg[0], w, (((1,), (1,)), ((), ())), preferred_element_type=jnp.float32
        ).astype(jnp.bfloat16)
        proj[...] += jnp.dot(tok_ref[:, cols], w, preferred_element_type=jnp.float32)

    def use_all(shard):
        def one(i, carry):
            use(shard, i)
            return carry

        lax.fori_loop(0, 4, one, 0)

    side = fsdp + 2 - 4 * y
    twin_shard = fsdp + 1 - 2 * c
    twin_side = side + 1 - 2 * c
    there_x, there_z, there = 2 * (1 - x) + z0, 2 * x + 1 - z0, 3 - here
    from_x, from_z, from_twin = [], [], []

    def pass_y(q):
        i = 2 * here + q
        from_y[q].wait_recv()
        from_x.append(send_w(side, i, 2 + q, over_x))
        from_z.append(send_w(side, i, 4 + q, over_z0))
        from_twin.append(send_w(side, i, 8 + q, twin))

    def pass_x(q):
        i = 2 * there_x + q
        from_x[q].wait_recv()
        from_z.append(send_w(side, i, 6 + q, over_z0))
        from_twin.append(send_w(side, i, 10 + q, twin))

    def pass_z(q):
        i = 2 * (there_z if q < 2 else there) + q % 2
        from_z[q].wait_recv()
        from_twin.append(send_w(side, i, 12 + q, twin))

    proj[...] = jnp.zeros_like(proj)
    blocks(1 - x, 1 - y)
    fa.launch(0, 0)
    fb.launch(0, 0)
    pass_y(0)
    blocks(1 - x, y)
    blocks(x, 1 - y)
    fa.launch(0, 1)
    fb.launch(0, 1)
    pass_y(1)
    blocks(x, y)
    fc.launch(0, 0)
    fd.launch(0, 0)

    def dequant_other(i, carry):
        other = (2 * here + 2 + i) % 8
        dequant(other)
        return carry

    lax.fori_loop(0, 6, dequant_other, 0)
    own = send(wbuf.at[fsdp], wbuf.at[fsdp], w_send.at[16], w_recv.at[16], twin)
    use_all(fsdp)
    pass_x(0)
    fa.take(0, 0)
    fb.take(0, 0)
    fc.launch(0, 1)
    fd.launch(0, 1)
    pass_z(0)
    own.wait_recv()
    use(twin_shard, 0)
    use(twin_shard, 1)
    pass_x(1)
    fa.take(0, 1)
    fb.take(0, 1)
    pass_z(1)
    use(twin_shard, 2)
    use(twin_shard, 3)
    fa.take(1, 0)
    fb.take(1, 0)
    use(side, here)
    fc.take(0, 0)
    fd.take(0, 0)
    fa.take(1, 1)
    fb.take(1, 1)
    pass_z(2)
    use(side, there_x)
    fa.take(2, 0)
    fb.take(2, 0)
    fc.take(0, 1)
    fd.take(0, 1)
    pass_z(3)
    use(side, there_z)
    fc.take(1, 0)
    fd.take(1, 0)
    use(side, there)
    fa.take(2, 1)
    fb.take(2, 1)
    for copy in from_twin[:2]:
        copy.wait_recv()
    use(twin_side, here)
    fc.take(1, 1)
    fd.take(1, 1)
    fc.take(2, 0)
    fd.take(2, 0)
    for copy in from_twin[2:]:
        copy.wait_recv()
    use(twin_side, there_x)
    use(twin_side, there_z)
    use(twin_side, there)
    for h in range(heads):
        cols = slice(h * HEAD_DIM, (h + 1) * HEAD_DIM)
        rot_ref[:, cols] = turn(proj[:, cols], 0, 1.0).astype(jnp.bfloat16)
    fa.finish(slice(0, quarter))
    fb.finish(slice(quarter, 2 * quarter))
    fc.take(2, 1)
    fd.take(2, 1)
    fc.finish(slice(2 * quarter, 3 * quarter))
    fd.finish(slice(3 * quarter, block))

    for group in range(4):
        group_copy(group // 2, group % 2).wait_send()
    for copy in started:
        copy.wait_send()


def fused_body(tokens, quant_weight, block_scales, key_grad):
    row_count, model = tokens.shape
    shard_rows, width = quant_weight.shape
    block = model // (lax.axis_size("rep") * lax.axis_size("fsdp"))
    bf16, f32 = jnp.bfloat16, jnp.float32
    vmem = pl.BlockSpec(memory_space=pltpu.VMEM)
    hbm = pl.BlockSpec(memory_space=pltpu.HBM)
    flows = [
        pltpu.VMEM((2,) * (4 - level) + (block // 4, width), bf16)
        for level in range(5)
        for _ in range(4)
    ]
    results = pl.pallas_call(
        fused_kernel,
        out_shape=[
            pltpu.VMEM((row_count, width), bf16),
            pltpu.VMEM((row_count, model), bf16),
            pltpu.VMEM((block, width), bf16),
        ],
        in_specs=[hbm, hbm, vmem, hbm],
        out_specs=[vmem] * 3,
        scratch_shapes=[
            pltpu.VMEM((row_count, model), bf16),
            pltpu.VMEM((shard_rows, width), bf16),
            pltpu.VMEM((row_count, width), bf16),
            pltpu.VMEM((row_count, width), bf16),
            pltpu.VMEM((4, 8, shard_rows // 8, width), bf16),
            pltpu.VMEM((2, 2, row_count, 4 * block), bf16),
            pltpu.VMEM((2, row_count, width), bf16),
            pltpu.VMEM((row_count, width), f32),
            pltpu.VMEM((2, row_count, HEAD_DIM), f32),
            pltpu.VMEM((2, row_count, HEAD_DIM), f32),
            *flows,
            pltpu.SemaphoreType.DMA((3,)),
            pltpu.SemaphoreType.DMA((8,)),
            pltpu.SemaphoreType.DMA((2,)),
            pltpu.SemaphoreType.DMA((17,)),
            pltpu.SemaphoreType.DMA((17,)),
            pltpu.SemaphoreType.DMA((32,)),
            pltpu.SemaphoreType.DMA((32,)),
        ],
        compiler_params=pltpu.CompilerParams(
            collective_id=0, has_side_effects=True, vmem_limit_bytes=56 * 1024 * 1024
        ),
    )(tokens, quant_weight, block_scales, key_grad)
    return pl.pallas_call(
        place_kernel,
        out_shape=[jax.ShapeDtypeStruct(value.shape, value.dtype) for value in results],
        in_specs=[vmem] * 3,
        out_specs=[hbm] * 3,
        scratch_shapes=[pltpu.SemaphoreType.DMA((3,))],
        compiler_params=pltpu.CompilerParams(vmem_limit_bytes=4 * 1024 * 1024),
    )(*results)


def place_kernel(rot_in, tg_in, wg_in, rot_out, tg_out, wg_out, sems):
    pairs = ((tg_in, tg_out), (rot_in, rot_out), (wg_in, wg_out))
    copies = [
        pltpu.make_async_copy(source, target, sems.at[i])
        for i, (source, target) in enumerate(pairs)
    ]
    for copy in copies:
        copy.start()
    for copy in copies:
        copy.wait()


def solution(mesh):
    paired = mesh.shape["rep"] == 8 and mesh.shape["fsdp"] == 4
    return jax.shard_map(
        fused_body if paired else body,
        mesh=mesh,
        in_specs=(P(("rep", "fsdp"), None), P("fsdp", None), P("fsdp"), P(("rep", "fsdp"), None)),
        out_specs=(P(("rep", "fsdp"), None), P(("rep", "fsdp"), None), P(("rep", "fsdp"), None)),
        check_vma=False,
    )
```

```python
import math

import jax
import jax.numpy as jnp
from jax import lax
from jax.experimental import pallas as pl
from jax.experimental.pallas import tpu as pltpu
from jax.sharding import PartitionSpec as P

HEAD_DIM = 128


rope_base = 10000.0


def dequantize(quant_weight, block_scales):
    rows_per_block = quant_weight.shape[0] // block_scales.shape[0]
    scaled = quant_weight.astype(jnp.float32).reshape(
        block_scales.shape[0], rows_per_block, quant_weight.shape[1]
    )
    scaled = scaled * block_scales.astype(jnp.float32)[:, None, None]
    return scaled.reshape(quant_weight.shape).astype(jnp.bfloat16)


def rotary(projected, positions, direction):
    half_size = HEAD_DIM // 2
    steps = jnp.arange(half_size, dtype=jnp.int32).astype(jnp.float32)
    frequency = jnp.exp(steps * (-2.0 * math.log(rope_base) / HEAD_DIM))
    angles = positions[:, None] * frequency[None, :]
    cosine = jnp.cos(angles)[:, None, :]
    sine_part = direction * jnp.sin(angles)[:, None, :]
    halves = projected.reshape(projected.shape[0], -1, 2, half_size)
    leading = halves[:, :, 0]
    trailing = halves[:, :, 1]
    turned = jnp.stack(
        [leading * cosine - trailing * sine_part, trailing * cosine + leading * sine_part], axis=2
    )
    return turned.reshape(projected.shape)


def partial_rows(source, proj_grad):
    return lax.dot_general(
        source, proj_grad, (((0,), (0,)), ((), ())), preferred_element_type=jnp.float32
    )


def body(tokens, quant_weight, block_scales, key_grad):
    row_count = tokens.shape[0]
    all_codes, all_scales = (
        lax.all_gather(quant_weight, "fsdp", axis=0, tiled=True),
        lax.all_gather(block_scales, "fsdp", axis=0, tiled=True),
    )
    weight = dequantize(all_codes, all_scales)
    positions = (
        lax.axis_index("fsdp") * row_count + jnp.arange(row_count, dtype=jnp.int32)
    ).astype(jnp.float32)
    projected = jnp.dot(tokens, weight, preferred_element_type=jnp.float32)
    rotated = rotary(projected, positions, 1.0).astype(jnp.bfloat16)
    proj_grad = rotary(key_grad.astype(jnp.float32), positions, -1.0).astype(jnp.bfloat16)
    token_grad = lax.dot_general(
        proj_grad, weight, (((1,), (1,)), ((), ())), preferred_element_type=jnp.float32
    ).astype(jnp.bfloat16)
    total_rows = weight.shape[0]
    fsdp_size = lax.axis_size("fsdp")
    rep_size = lax.axis_size("rep")
    share = total_rows // (fsdp_size * rep_size)
    reordered = (
        tokens.reshape(row_count, rep_size, fsdp_size, share)
        .transpose(0, 2, 1, 3)
        .reshape(row_count, total_rows)
    )
    group_sum = lax.psum_scatter(
        partial_rows(reordered, proj_grad).astype(jnp.bfloat16),
        "fsdp",
        scatter_dimension=0,
        tiled=True,
    ).astype(jnp.float32)
    summed = lax.psum_scatter(group_sum, "rep", scatter_dimension=0, tiled=True)
    weight_grad = (summed * (1.0 / math.sqrt(row_count * fsdp_size * rep_size))).astype(
        jnp.bfloat16
    )
    return (rotated, token_grad, weight_grad)


MESH = pl.DeviceIdType.MESH


def fused_kernel(
    tok_hbm, quant_hbm, scale_ref, kg_hbm,
    rot_ref, tg_ref, wg_ref,
    tok_ref, quant_ref, kg_ref, kg_twin,
    wbuf, tok_twin, pg, proj, cos_t, sin_t,
    sa, sb, sc, sd, a1, b1, c1, d1, a2, b2, c2, d2, a3, b3, c3, d3, a4, b4, c4, d4,
    load_sem, tok_sem, pg_sem, w_send, w_recv, rs_send, rs_recv,
):
    rep, fsdp = lax.axis_index("rep"), lax.axis_index("fsdp")
    x, z0, z1 = rep % 2, (rep // 2) % 2, rep // 4
    y, c = fsdp // 2, fsdp % 2
    twin = (rep, fsdp + 1 - 2 * c)
    over_y = (rep, fsdp + 2 - 4 * y)
    over_x = (rep + 1 - 2 * x, fsdp)
    over_z0 = (rep + 2 - 4 * z0, fsdp)
    over_z1 = (rep + 4 - 8 * z1, fsdp)
    row_count, width = kg_ref.shape
    shard_rows = quant_ref.shape[0]
    piece = shard_rows // 4
    part = shard_rows // 8
    block = wg_ref.shape[0]
    here = 2 * x + z0

    load_quant = pltpu.make_async_copy(quant_hbm, quant_ref, load_sem.at[0])
    load_quant.start()
    load_kg = pltpu.make_async_copy(kg_hbm, kg_ref, load_sem.at[1])
    load_kg.start()
    load_tok = pltpu.make_async_copy(tok_hbm, tok_ref, load_sem.at[2])
    load_tok.start()

    barrier = pltpu.get_barrier_semaphore()
    for other in (twin, over_y, over_x, over_z0, over_z1):
        pl.semaphore_signal(barrier, inc=1, device_id=other, device_id_type=MESH)

    def dequant(i):
        rows = pl.ds(pl.multiple_of(i * part, part), part)
        n_blocks = scale_ref.shape[0]
        per_block = shard_rows // n_blocks
        owner = (i * part + lax.broadcasted_iota(jnp.int32, (part, n_blocks), 0)) // per_block
        lane = lax.broadcasted_iota(jnp.int32, (part, n_blocks), 1)
        picked = jnp.where(owner == lane, scale_ref[...].astype(jnp.float32).reshape(1, n_blocks), 0.0)
        column = jnp.sum(picked, axis=1, keepdims=True)
        wbuf[fsdp, i] = (quant_ref[rows, :].astype(jnp.float32) * column).astype(jnp.bfloat16)

    load_quant.wait()
    dequant(2 * here)
    dequant(2 * here + 1)
    pl.semaphore_wait(barrier, 5)

    started = []

    def send(src, dst, send_sem, recv_sem, to):
        copy = pltpu.make_async_remote_copy(
            src_ref=src, dst_ref=dst, send_sem=send_sem, recv_sem=recv_sem,
            device_id=to, device_id_type=MESH,
        )
        copy.start()
        started.append(copy)
        return copy

    def send_w(shard, i, slot, to):
        return send(
            wbuf.at[shard, i], wbuf.at[shard, i], w_send.at[slot], w_recv.at[slot], to
        )

    def w_copy(shard, i, slot, to):
        return pltpu.make_async_remote_copy(
            src_ref=wbuf.at[shard, i], dst_ref=wbuf.at[shard, i],
            send_sem=w_send.at[slot], recv_sem=w_recv.at[slot],
            device_id=to, device_id_type=MESH,
        )

    from_y = [send_w(fsdp, 2 * here + q, q, over_y) for q in range(2)]

    def send_tokens(bx, by):
        group = 2 * bx + by
        for k in range(4):
            col = pl.multiple_of(((k % 2 * 8 + k // 2 * 4 + group) * 2 + 1 - c) * block, block)
            pltpu.make_async_remote_copy(
                src_ref=tok_ref.at[:, pl.ds(col, block)],
                dst_ref=tok_twin.at[bx, by, :, pl.ds(k * block, block)],
                send_sem=tok_sem.at[group], recv_sem=tok_sem.at[4 + group],
                device_id=twin, device_id_type=MESH,
            ).start()

    def group_copy(bx, by):
        group = 2 * bx + by
        return pltpu.make_async_remote_copy(
            src_ref=tok_twin.at[bx, by], dst_ref=tok_twin.at[bx, by],
            send_sem=tok_sem.at[group], recv_sem=tok_sem.at[4 + group],
            device_id=twin, device_id_type=MESH,
        )

    load_kg.wait()
    kg_copy = send(kg_ref, kg_twin, pg_sem.at[0], pg_sem.at[1], twin)
    load_tok.wait()
    send_tokens(1 - x, 1 - y)
    send_tokens(1 - x, y)
    send_tokens(x, 1 - y)
    send_tokens(x, y)

    half = HEAD_DIM // 2
    low_rows = 8
    high_rows = row_count // low_rows

    def angles(rows, first, step):
        shape = (rows, HEAD_DIM)
        steps = (lax.broadcasted_iota(jnp.int32, shape, 1) % half).astype(jnp.float32)
        frequency = jnp.exp(steps * (-2.0 * math.log(rope_base) / HEAD_DIM))
        place = first + step * lax.broadcasted_iota(jnp.int32, shape, 0)
        return place.astype(jnp.float32) * frequency

    low = angles(low_rows, 0, 1)
    cos_low, sin_low = jnp.cos(low), jnp.sin(low)
    leading = lax.broadcasted_iota(jnp.int32, (low_rows, HEAD_DIM), 1) < half
    heads = width // HEAD_DIM

    def turn(value, whose, direction):
        flipped = pltpu.roll(value, half, 1) * (direction * sin_t[whose])
        return value * cos_t[whose] + flipped

    def make_pg(whose, owner, source):
        high = angles(high_rows, owner * row_count, low_rows)
        cos_high, sin_high = jnp.cos(high), jnp.sin(high)
        for i in range(high_rows):
            rows = slice(i * low_rows, (i + 1) * low_rows)
            ch, sh = cos_high[i : i + 1], sin_high[i : i + 1]
            cos_t[whose, rows, :] = ch * cos_low - sh * sin_low
            sine = sh * cos_low + ch * sin_low
            sin_t[whose, rows, :] = jnp.where(leading, -sine, sine)
        for h in range(heads):
            cols = slice(h * HEAD_DIM, (h + 1) * HEAD_DIM)
            value = source[:, cols].astype(jnp.float32)
            pg[whose, :, cols] = turn(value, whose, -1.0).astype(jnp.bfloat16)

    make_pg(0, fsdp, kg_ref)
    kg_copy.wait_recv()
    make_pg(1, fsdp + 1 - 2 * c, kg_twin)

    quarter = block // 4

    def blocks(bx, by):
        group_copy(bx, by).wait_recv()
        own_columns = [
            tok_ref[:, pl.ds(pl.multiple_of(((k % 2 * 8 + k // 2 * 4 + 2 * bx + by) * 2 + c) * block, block), block)]
            for k in range(4)
        ]
        left = jnp.concatenate(
            [jnp.concatenate(own_columns, axis=1), tok_twin[bx, by]], axis=0
        )
        right = pg[...].reshape(2 * row_count, width)
        total = lax.dot_general(
            left, right, (((0,), (0,)), ((), ())), preferred_element_type=jnp.float32
        ).astype(jnp.bfloat16).reshape(2, 2, 4, quarter, width)
        sa[bx, by] = total[:, :, 0]
        sb[by, bx] = total[:, :, 1]
        for bz0 in range(2):
            sc[bx, bz0, by] = total[bz0, :, 2]
            sd[by, bz0, bx] = total[bz0, :, 3]

    class Flow:
        def __init__(self, index, bits, others, bufs):
            self.index, self.bits, self.others, self.bufs = index, bits, others, bufs
            self.copies = {}

        def launch(self, stage, turn_of):
            bits, bufs = self.bits, self.bufs
            slot = self.index * 8 + stage * 2 + turn_of
            sems = (rs_send.at[slot], rs_recv.at[slot], self.others[stage])
            lead = 1 - bits[stage]
            if stage == 3:
                src, dst = bufs[3].at[lead], bufs[4]
            else:
                sub = 1 - bits[stage + 1] if turn_of == 0 else bits[stage + 1]
                src, dst = bufs[stage].at[lead, sub], bufs[stage + 1].at[sub]
            self.copies[stage, turn_of] = send(src, dst, *sems)

        def take(self, stage, turn_of):
            bits, bufs = self.bits, self.bufs
            self.copies[stage, turn_of].wait_recv()
            sub = 1 - bits[stage + 1] if turn_of == 0 else bits[stage + 1]
            mine = bufs[stage][bits[stage], sub].astype(jnp.float32)
            bufs[stage + 1][sub] = (
                bufs[stage + 1][sub].astype(jnp.float32) + mine
            ).astype(jnp.bfloat16)
            if turn_of == 0:
                self.launch(stage + 1, 0)
                if stage + 1 < 3:
                    self.launch(stage + 1, 1)

        def finish(self, rows):
            bits, bufs = self.bits, self.bufs
            self.copies[3, 0].wait_recv()
            total = bufs[4][...].astype(jnp.float32) + bufs[3][bits[3]].astype(jnp.float32)
            count = row_count * lax.axis_size("rep") * lax.axis_size("fsdp")
            wg_ref[rows, :] = (total * (1.0 / math.sqrt(count))).astype(jnp.bfloat16)

    x_first = ((x, y, z0, z1), (over_x, over_y, over_z0, over_z1))
    y_first = ((y, x, z0, z1), (over_y, over_x, over_z0, over_z1))
    fa = Flow(0, *x_first, (sa, a1, a2, a3, a4))
    fb = Flow(1, *y_first, (sb, b1, b2, b3, b4))
    x_then_z = ((x, z0, y, z1), (over_x, over_z0, over_y, over_z1))
    y_then_z = ((y, z0, x, z1), (over_y, over_z0, over_x, over_z1))
    fc = Flow(2, *x_then_z, (sc, c1, c2, c3, c4))
    fd = Flow(3, *y_then_z, (sd, d1, d2, d3, d4))

    def use(shard, at):
        col = pl.multiple_of(shard * shard_rows + at * piece, piece)
        cols = pl.ds(col, piece)
        w = wbuf[shard, pl.ds(2 * at, 2)].reshape(piece, width)
        tg_ref[:, cols] = lax.dot_general(
            pg[0], w, (((1,), (1,)), ((), ())), preferred_element_type=jnp.float32
        ).astype(jnp.bfloat16)
        proj[...] += jnp.dot(tok_ref[:, cols], w, preferred_element_type=jnp.float32)

    def use_all(shard):
        def one(i, carry):
            use(shard, i)
            return carry

        lax.fori_loop(0, 4, one, 0)

    side = fsdp + 2 - 4 * y
    twin_shard = fsdp + 1 - 2 * c
    twin_side = side + 1 - 2 * c
    there_x, there_z, there = 2 * (1 - x) + z0, 2 * x + 1 - z0, 3 - here
    from_x, from_z, from_twin = [], [], []

    def pass_y(q):
        i = 2 * here + q
        from_y[q].wait_recv()
        from_x.append(send_w(side, i, 2 + q, over_x))
        from_z.append(send_w(side, i, 4 + q, over_z0))
        from_twin.append(send_w(side, i, 8 + q, twin))

    def pass_x(q):
        i = 2 * there_x + q
        from_x[q].wait_recv()
        send_w(side, i, 10 + q, twin)

        @pl.when(c == 1)
        def _():
            w_copy(side, i, 6 + q, over_z0).start()

    def lift(q):
        i = 2 * there_x + q

        @pl.when(c == 1)
        def _():
            w_copy(twin_side, i, 10 + q, twin).wait_recv()
            w_copy(twin_side, i, 17 + q, over_z0).start()

    def pass_z(q):
        from_z[q].wait_recv()
        from_twin.append(send_w(side, 2 * there_z + q, 12 + q, twin))

    def pass_z_both(q):
        i = 2 * there + q

        @pl.when(c == 1)
        def _():
            w_copy(side, i, 6 + q, over_z0).wait_recv()
            w_copy(side, i, 14 + q, twin).start()
            w_copy(twin_side, i, 17 + q, over_z0).wait_recv()
            w_copy(twin_side, i, 19 + q, twin).start()

    proj[...] = jnp.zeros_like(proj)
    blocks(1 - x, 1 - y)
    fa.launch(0, 0)
    fb.launch(0, 0)
    pass_y(0)
    blocks(1 - x, y)
    blocks(x, 1 - y)
    fa.launch(0, 1)
    fb.launch(0, 1)
    pass_y(1)
    blocks(x, y)
    def dequant_other(i, carry):
        other = (2 * here + 2 + i) % 8
        dequant(other)
        return carry

    lax.fori_loop(0, 6, dequant_other, 0)
    own = send(wbuf.at[fsdp], wbuf.at[fsdp], w_send.at[16], w_recv.at[16], twin)
    use_all(fsdp)
    pass_x(0)
    fa.take(0, 0)
    fb.take(0, 0)
    for turn_of in range(2):
        fc.launch(0, turn_of)
        fd.launch(0, turn_of)
    pass_z(0)
    lift(0)
    pass_x(1)
    own.wait_recv()
    use(twin_shard, 0)
    use(twin_shard, 1)
    pass_z(1)
    fa.take(0, 1)
    fb.take(0, 1)
    lift(1)
    use(twin_shard, 2)
    use(twin_shard, 3)
    fa.take(1, 0)
    fb.take(1, 0)
    use(side, here)
    fc.take(0, 0)
    fd.take(0, 0)
    fa.take(1, 1)
    fb.take(1, 1)
    pass_z_both(0)
    use(side, there_x)
    use(side, there_z)
    fa.take(2, 0)
    fb.take(2, 0)
    fc.take(0, 1)
    fd.take(0, 1)
    pass_z_both(1)
    for copy in from_twin[:2]:
        copy.wait_recv()
    use(twin_side, here)
    fc.take(1, 0)
    fd.take(1, 0)
    fa.take(2, 1)
    fb.take(2, 1)
    for copy in from_twin[2:]:
        copy.wait_recv()
    use(twin_side, there_z)
    fc.take(1, 1)
    fd.take(1, 1)
    fc.take(2, 0)
    fd.take(2, 0)

    @pl.when(c == 0)
    def _():
        for q in range(2):
            w_copy(twin_side, 2 * there_x + q, 10 + q, twin).wait_recv()
            w_copy(twin_side, 2 * there + q, 14 + q, twin).wait_recv()
            w_copy(side, 2 * there + q, 19 + q, twin).wait_recv()

    use(twin_side, there_x)
    use(side, there)
    use(twin_side, there)
    for h in range(heads):
        cols = slice(h * HEAD_DIM, (h + 1) * HEAD_DIM)
        rot_ref[:, cols] = turn(proj[:, cols], 0, 1.0).astype(jnp.bfloat16)
    fa.finish(slice(0, quarter))
    fb.finish(slice(quarter, 2 * quarter))
    fc.take(2, 1)
    fd.take(2, 1)
    fc.finish(slice(2 * quarter, 3 * quarter))
    fd.finish(slice(3 * quarter, block))

    @pl.when(c == 1)
    def _():
        for q in range(2):
            w_copy(side, 2 * there_x + q, 6 + q, over_z0).wait_send()
            w_copy(twin_side, 2 * there_x + q, 17 + q, over_z0).wait_send()
            w_copy(side, 2 * there + q, 14 + q, twin).wait_send()
            w_copy(twin_side, 2 * there + q, 19 + q, twin).wait_send()

    for group in range(4):
        group_copy(group // 2, group % 2).wait_send()
    for copy in started:
        copy.wait_send()


def fused_body(tokens, quant_weight, block_scales, key_grad):
    row_count, model = tokens.shape
    shard_rows, width = quant_weight.shape
    block = model // (lax.axis_size("rep") * lax.axis_size("fsdp"))
    bf16, f32 = jnp.bfloat16, jnp.float32
    vmem = pl.BlockSpec(memory_space=pltpu.VMEM)
    hbm = pl.BlockSpec(memory_space=pltpu.HBM)
    flows = [
        pltpu.VMEM((2,) * (4 - level) + (block // 4, width), bf16)
        for level in range(5)
        for _ in range(4)
    ]
    results = pl.pallas_call(
        fused_kernel,
        out_shape=[
            pltpu.VMEM((row_count, width), bf16),
            pltpu.VMEM((row_count, model), bf16),
            pltpu.VMEM((block, width), bf16),
        ],
        in_specs=[hbm, hbm, vmem, hbm],
        out_specs=[vmem] * 3,
        scratch_shapes=[
            pltpu.VMEM((row_count, model), bf16),
            pltpu.VMEM((shard_rows, width), bf16),
            pltpu.VMEM((row_count, width), bf16),
            pltpu.VMEM((row_count, width), bf16),
            pltpu.VMEM((4, 8, shard_rows // 8, width), bf16),
            pltpu.VMEM((2, 2, row_count, 4 * block), bf16),
            pltpu.VMEM((2, row_count, width), bf16),
            pltpu.VMEM((row_count, width), f32),
            pltpu.VMEM((2, row_count, HEAD_DIM), f32),
            pltpu.VMEM((2, row_count, HEAD_DIM), f32),
            *flows,
            pltpu.SemaphoreType.DMA((3,)),
            pltpu.SemaphoreType.DMA((8,)),
            pltpu.SemaphoreType.DMA((2,)),
            pltpu.SemaphoreType.DMA((21,)),
            pltpu.SemaphoreType.DMA((21,)),
            pltpu.SemaphoreType.DMA((32,)),
            pltpu.SemaphoreType.DMA((32,)),
        ],
        compiler_params=pltpu.CompilerParams(
            collective_id=0, has_side_effects=True, vmem_limit_bytes=56 * 1024 * 1024
        ),
    )(tokens, quant_weight, block_scales, key_grad)
    return pl.pallas_call(
        place_kernel,
        out_shape=[jax.ShapeDtypeStruct(value.shape, value.dtype) for value in results],
        in_specs=[vmem] * 3,
        out_specs=[hbm] * 3,
        scratch_shapes=[pltpu.SemaphoreType.DMA((3,))],
        compiler_params=pltpu.CompilerParams(vmem_limit_bytes=4 * 1024 * 1024),
    )(*results)


def place_kernel(rot_in, tg_in, wg_in, rot_out, tg_out, wg_out, sems):
    pairs = ((tg_in, tg_out), (rot_in, rot_out), (wg_in, wg_out))
    copies = [
        pltpu.make_async_copy(source, target, sems.at[i])
        for i, (source, target) in enumerate(pairs)
    ]
    for copy in copies:
        copy.start()
    for copy in copies:
        copy.wait()


def solution(mesh):
    paired = mesh.shape["rep"] == 8 and mesh.shape["fsdp"] == 4
    return jax.shard_map(
        fused_body if paired else body,
        mesh=mesh,
        in_specs=(P(("rep", "fsdp"), None), P("fsdp", None), P("fsdp"), P(("rep", "fsdp"), None)),
        out_specs=(P(("rep", "fsdp"), None), P(("rep", "fsdp"), None), P(("rep", "fsdp"), None)),
        check_vma=False,
    )
```

```python
import math

import jax
import jax.numpy as jnp
from jax import lax
from jax.experimental import pallas as pl
from jax.experimental.pallas import tpu as pltpu
from jax.sharding import PartitionSpec as P

HEAD_DIM = 128


rope_base = 10000.0


def dequantize(quant_weight, block_scales):
    rows_per_block = quant_weight.shape[0] // block_scales.shape[0]
    scaled = quant_weight.astype(jnp.float32).reshape(
        block_scales.shape[0], rows_per_block, quant_weight.shape[1]
    )
    scaled = scaled * block_scales.astype(jnp.float32)[:, None, None]
    return scaled.reshape(quant_weight.shape).astype(jnp.bfloat16)


def rotary(projected, positions, direction):
    half_size = HEAD_DIM // 2
    steps = jnp.arange(half_size, dtype=jnp.int32).astype(jnp.float32)
    frequency = jnp.exp(steps * (-2.0 * math.log(rope_base) / HEAD_DIM))
    angles = positions[:, None] * frequency[None, :]
    cosine = jnp.cos(angles)[:, None, :]
    sine_part = direction * jnp.sin(angles)[:, None, :]
    halves = projected.reshape(projected.shape[0], -1, 2, half_size)
    leading = halves[:, :, 0]
    trailing = halves[:, :, 1]
    turned = jnp.stack(
        [leading * cosine - trailing * sine_part, trailing * cosine + leading * sine_part], axis=2
    )
    return turned.reshape(projected.shape)


def partial_rows(source, proj_grad):
    return lax.dot_general(
        source, proj_grad, (((0,), (0,)), ((), ())), preferred_element_type=jnp.float32
    )


def body(tokens, quant_weight, block_scales, key_grad):
    row_count = tokens.shape[0]
    all_codes, all_scales = (
        lax.all_gather(quant_weight, "fsdp", axis=0, tiled=True),
        lax.all_gather(block_scales, "fsdp", axis=0, tiled=True),
    )
    weight = dequantize(all_codes, all_scales)
    positions = (
        lax.axis_index("fsdp") * row_count + jnp.arange(row_count, dtype=jnp.int32)
    ).astype(jnp.float32)
    projected = jnp.dot(tokens, weight, preferred_element_type=jnp.float32)
    rotated = rotary(projected, positions, 1.0).astype(jnp.bfloat16)
    proj_grad = rotary(key_grad.astype(jnp.float32), positions, -1.0).astype(jnp.bfloat16)
    token_grad = lax.dot_general(
        proj_grad, weight, (((1,), (1,)), ((), ())), preferred_element_type=jnp.float32
    ).astype(jnp.bfloat16)
    total_rows = weight.shape[0]
    fsdp_size = lax.axis_size("fsdp")
    rep_size = lax.axis_size("rep")
    share = total_rows // (fsdp_size * rep_size)
    reordered = (
        tokens.reshape(row_count, rep_size, fsdp_size, share)
        .transpose(0, 2, 1, 3)
        .reshape(row_count, total_rows)
    )
    group_sum = lax.psum_scatter(
        partial_rows(reordered, proj_grad).astype(jnp.bfloat16),
        "fsdp",
        scatter_dimension=0,
        tiled=True,
    ).astype(jnp.float32)
    summed = lax.psum_scatter(group_sum, "rep", scatter_dimension=0, tiled=True)
    weight_grad = (summed * (1.0 / math.sqrt(row_count * fsdp_size * rep_size))).astype(
        jnp.bfloat16
    )
    return (rotated, token_grad, weight_grad)


MESH = pl.DeviceIdType.MESH


def fused_kernel(
    tok_hbm, quant_hbm, scale_ref, kg_hbm,
    rot_ref, tg_ref, wg_ref,
    tok_ref, quant_ref, kg_ref, kg_twin,
    wbuf, tok_twin, pg, proj, cos_t, sin_t,
    sa, sb, sc, sd, a1, b1, c1, d1, a2, b2, c2, d2, a3, b3, c3, d3, a4, b4, c4, d4,
    load_sem, tok_sem, pg_sem, w_send, w_recv, rs_send, rs_recv,
):
    rep, fsdp = lax.axis_index("rep"), lax.axis_index("fsdp")
    x, z0, z1 = rep % 2, (rep // 2) % 2, rep // 4
    y, c = fsdp // 2, fsdp % 2
    twin = (rep, fsdp + 1 - 2 * c)
    over_y = (rep, fsdp + 2 - 4 * y)
    over_x = (rep + 1 - 2 * x, fsdp)
    over_z0 = (rep + 2 - 4 * z0, fsdp)
    over_z1 = (rep + 4 - 8 * z1, fsdp)
    row_count, width = kg_ref.shape
    shard_rows = quant_ref.shape[0]
    piece = shard_rows // 4
    part = shard_rows // 8
    block = wg_ref.shape[0]
    here = 2 * x + z0

    load_quant = pltpu.make_async_copy(quant_hbm, quant_ref, load_sem.at[0])
    load_quant.start()
    load_kg = pltpu.make_async_copy(kg_hbm, kg_ref, load_sem.at[1])
    load_kg.start()
    load_tok = pltpu.make_async_copy(tok_hbm, tok_ref, load_sem.at[2])
    load_tok.start()

    barrier = pltpu.get_barrier_semaphore()
    for other in (twin, over_y, over_x, over_z0, over_z1):
        pl.semaphore_signal(barrier, inc=1, device_id=other, device_id_type=MESH)

    def dequant(i):
        rows = pl.ds(pl.multiple_of(i * part, part), part)
        n_blocks = scale_ref.shape[0]
        per_block = shard_rows // n_blocks
        owner = (i * part + lax.broadcasted_iota(jnp.int32, (part, n_blocks), 0)) // per_block
        lane = lax.broadcasted_iota(jnp.int32, (part, n_blocks), 1)
        picked = jnp.where(owner == lane, scale_ref[...].astype(jnp.float32).reshape(1, n_blocks), 0.0)
        column = jnp.sum(picked, axis=1, keepdims=True)
        wbuf[fsdp, i] = (quant_ref[rows, :].astype(jnp.float32) * column).astype(jnp.bfloat16)

    load_quant.wait()
    dequant(2 * here)
    dequant(2 * here + 1)
    pl.semaphore_wait(barrier, 5)

    started = []

    def send(src, dst, send_sem, recv_sem, to):
        copy = pltpu.make_async_remote_copy(
            src_ref=src, dst_ref=dst, send_sem=send_sem, recv_sem=recv_sem,
            device_id=to, device_id_type=MESH,
        )
        copy.start()
        started.append(copy)
        return copy

    def send_w(shard, i, slot, to):
        return send(
            wbuf.at[shard, i], wbuf.at[shard, i], w_send.at[slot], w_recv.at[slot], to
        )

    from_y = [send_w(fsdp, 2 * here + q, q, over_y) for q in range(2)]

    def send_tokens(bx, by):
        group = 2 * bx + by
        for k in range(4):
            col = pl.multiple_of(((k % 2 * 8 + k // 2 * 4 + group) * 2 + 1 - c) * block, block)
            pltpu.make_async_remote_copy(
                src_ref=tok_ref.at[:, pl.ds(col, block)],
                dst_ref=tok_twin.at[bx, by, :, pl.ds(k * block, block)],
                send_sem=tok_sem.at[group], recv_sem=tok_sem.at[4 + group],
                device_id=twin, device_id_type=MESH,
            ).start()

    def group_copy(bx, by):
        group = 2 * bx + by
        return pltpu.make_async_remote_copy(
            src_ref=tok_twin.at[bx, by], dst_ref=tok_twin.at[bx, by],
            send_sem=tok_sem.at[group], recv_sem=tok_sem.at[4 + group],
            device_id=twin, device_id_type=MESH,
        )

    load_kg.wait()
    kg_copy = send(kg_ref, kg_twin, pg_sem.at[0], pg_sem.at[1], twin)
    load_tok.wait()
    send_tokens(1 - x, 1 - y)
    send_tokens(1 - x, y)
    send_tokens(x, 1 - y)
    send_tokens(x, y)

    half = HEAD_DIM // 2
    low_rows = 8
    high_rows = row_count // low_rows

    def angles(rows, first, step):
        shape = (rows, HEAD_DIM)
        steps = (lax.broadcasted_iota(jnp.int32, shape, 1) % half).astype(jnp.float32)
        frequency = jnp.exp(steps * (-2.0 * math.log(rope_base) / HEAD_DIM))
        place = first + step * lax.broadcasted_iota(jnp.int32, shape, 0)
        return place.astype(jnp.float32) * frequency

    low = angles(low_rows, 0, 1)
    cos_low, sin_low = jnp.cos(low), jnp.sin(low)
    leading = lax.broadcasted_iota(jnp.int32, (low_rows, HEAD_DIM), 1) < half
    heads = width // HEAD_DIM

    def turn(value, whose, direction):
        flipped = pltpu.roll(value, half, 1) * (direction * sin_t[whose])
        return value * cos_t[whose] + flipped

    def make_pg(whose, owner, source):
        high = angles(high_rows, owner * row_count, low_rows)
        cos_high, sin_high = jnp.cos(high), jnp.sin(high)
        for i in range(high_rows):
            rows = slice(i * low_rows, (i + 1) * low_rows)
            ch, sh = cos_high[i : i + 1], sin_high[i : i + 1]
            cos_t[whose, rows, :] = ch * cos_low - sh * sin_low
            sine = sh * cos_low + ch * sin_low
            sin_t[whose, rows, :] = jnp.where(leading, -sine, sine)
        for h in range(heads):
            cols = slice(h * HEAD_DIM, (h + 1) * HEAD_DIM)
            value = source[:, cols].astype(jnp.float32)
            pg[whose, :, cols] = turn(value, whose, -1.0).astype(jnp.bfloat16)

    make_pg(0, fsdp, kg_ref)
    kg_copy.wait_recv()
    make_pg(1, fsdp + 1 - 2 * c, kg_twin)

    quarter = block // 4

    def blocks(bx, by):
        group_copy(bx, by).wait_recv()
        own_columns = [
            tok_ref[:, pl.ds(pl.multiple_of(((k % 2 * 8 + k // 2 * 4 + 2 * bx + by) * 2 + c) * block, block), block)]
            for k in range(4)
        ]
        left = jnp.concatenate(
            [jnp.concatenate(own_columns, axis=1), tok_twin[bx, by]], axis=0
        )
        right = pg[...].reshape(2 * row_count, width)
        total = lax.dot_general(
            left, right, (((0,), (0,)), ((), ())), preferred_element_type=jnp.float32
        ).astype(jnp.bfloat16).reshape(2, 2, 4, quarter, width)
        sa[bx, by] = total[:, :, 0]
        sb[by, bx] = total[:, :, 1]
        for bz0 in range(2):
            sc[bx, bz0, by] = total[bz0, :, 2]
            sd[by, bz0, bx] = total[bz0, :, 3]

    class Flow:
        def __init__(self, index, bits, others, bufs):
            self.index, self.bits, self.others, self.bufs = index, bits, others, bufs
            self.copies = {}

        def launch(self, stage, turn_of):
            bits, bufs = self.bits, self.bufs
            slot = self.index * 8 + stage * 2 + turn_of
            sems = (rs_send.at[slot], rs_recv.at[slot], self.others[stage])
            lead = 1 - bits[stage]
            if stage == 3:
                src, dst = bufs[3].at[lead], bufs[4]
            else:
                sub = 1 - bits[stage + 1] if turn_of == 0 else bits[stage + 1]
                src, dst = bufs[stage].at[lead, sub], bufs[stage + 1].at[sub]
            self.copies[stage, turn_of] = send(src, dst, *sems)

        def take(self, stage, turn_of):
            bits, bufs = self.bits, self.bufs
            self.copies[stage, turn_of].wait_recv()
            sub = 1 - bits[stage + 1] if turn_of == 0 else bits[stage + 1]
            mine = bufs[stage][bits[stage], sub].astype(jnp.float32)
            bufs[stage + 1][sub] = (
                bufs[stage + 1][sub].astype(jnp.float32) + mine
            ).astype(jnp.bfloat16)
            if turn_of == 0:
                self.launch(stage + 1, 0)
                if stage + 1 < 3:
                    self.launch(stage + 1, 1)

        def finish(self, rows):
            bits, bufs = self.bits, self.bufs
            self.copies[3, 0].wait_recv()
            total = bufs[4][...].astype(jnp.float32) + bufs[3][bits[3]].astype(jnp.float32)
            count = row_count * lax.axis_size("rep") * lax.axis_size("fsdp")
            wg_ref[rows, :] = (total * (1.0 / math.sqrt(count))).astype(jnp.bfloat16)

    x_first = ((x, y, z0, z1), (over_x, over_y, over_z0, over_z1))
    y_first = ((y, x, z0, z1), (over_y, over_x, over_z0, over_z1))
    fa = Flow(0, *x_first, (sa, a1, a2, a3, a4))
    fb = Flow(1, *y_first, (sb, b1, b2, b3, b4))
    x_then_z = ((x, z0, y, z1), (over_x, over_z0, over_y, over_z1))
    y_then_z = ((y, z0, x, z1), (over_y, over_z0, over_x, over_z1))
    fc = Flow(2, *x_then_z, (sc, c1, c2, c3, c4))
    fd = Flow(3, *y_then_z, (sd, d1, d2, d3, d4))

    def use(shard, at):
        col = pl.multiple_of(shard * shard_rows + at * piece, piece)
        cols = pl.ds(col, piece)
        w = wbuf[shard, pl.ds(2 * at, 2)].reshape(piece, width)
        tg_ref[:, cols] = lax.dot_general(
            pg[0], w, (((1,), (1,)), ((), ())), preferred_element_type=jnp.float32
        ).astype(jnp.bfloat16)
        proj[...] += jnp.dot(tok_ref[:, cols], w, preferred_element_type=jnp.float32)

    def use_all(shard):
        def one(i, carry):
            use(shard, i)
            return carry

        lax.fori_loop(0, 4, one, 0)

    side = fsdp + 2 - 4 * y
    twin_shard = fsdp + 1 - 2 * c
    twin_side = side + 1 - 2 * c
    there_x, there_z, there = 2 * (1 - x) + z0, 2 * x + 1 - z0, 3 - here
    from_x, from_z, from_twin = [], [], []

    def pass_y(q):
        i = 2 * here + q
        from_y[q].wait_recv()
        from_x.append(send_w(side, i, 2 + q, over_x))
        from_z.append(send_w(side, i, 4 + q, over_z0))
        from_twin.append(send_w(side, i, 8 + q, twin))

    def pass_x(q):
        i = 2 * there_x + q
        from_x[q].wait_recv()
        from_z.append(send_w(side, i, 6 + q, over_z0))
        from_twin.append(send_w(side, i, 10 + q, twin))

    def pass_z(q):
        i = 2 * (there_z if q < 2 else there) + q % 2
        from_z[q].wait_recv()
        from_twin.append(send_w(side, i, 12 + q, twin))

    proj[...] = jnp.zeros_like(proj)
    blocks(1 - x, 1 - y)
    fa.launch(0, 0)
    fb.launch(0, 0)
    pass_y(0)
    blocks(1 - x, y)
    blocks(x, 1 - y)
    pass_y(1)
    fa.launch(0, 1)
    fb.launch(0, 1)
    blocks(x, y)
    def dequant_other(i, carry):
        other = (2 * here + 2 + i) % 8
        dequant(other)
        return carry

    lax.fori_loop(0, 6, dequant_other, 0)
    own = send(wbuf.at[fsdp], wbuf.at[fsdp], w_send.at[16], w_recv.at[16], twin)
    use_all(fsdp)
    pass_x(0)
    fa.take(0, 0)
    fc.launch(0, 0)
    fb.take(0, 0)
    fd.launch(0, 0)
    pass_z(0)
    pass_x(1)
    own.wait_recv()
    use(twin_shard, 0)
    use(twin_shard, 1)
    pass_z(1)
    fa.take(0, 1)
    fc.launch(0, 1)
    fb.take(0, 1)
    fd.launch(0, 1)
    use(twin_shard, 2)
    use(twin_shard, 3)
    fa.take(1, 0)
    fb.take(1, 0)
    use(side, here)
    pass_z(2)
    fc.take(0, 0)
    fd.take(0, 0)
    fa.take(1, 1)
    fb.take(1, 1)
    pass_z(3)
    use(side, there_x)
    use(side, there_z)
    fa.take(2, 0)
    fb.take(2, 0)
    fc.take(0, 1)
    fd.take(0, 1)
    use(side, there)
    for copy in from_twin[:2]:
        copy.wait_recv()
    use(twin_side, here)
    fc.take(1, 0)
    fd.take(1, 0)
    fa.take(2, 1)
    fb.take(2, 1)
    for copy in from_twin[2:]:
        copy.wait_recv()
    use(twin_side, there_x)
    use(twin_side, there_z)
    fc.take(1, 1)
    fd.take(1, 1)
    use(twin_side, there)
    fc.take(2, 0)
    fd.take(2, 0)
    for h in range(heads):
        cols = slice(h * HEAD_DIM, (h + 1) * HEAD_DIM)
        rot_ref[:, cols] = turn(proj[:, cols], 0, 1.0).astype(jnp.bfloat16)
    fa.finish(slice(0, quarter))
    fb.finish(slice(quarter, 2 * quarter))
    fc.take(2, 1)
    fd.take(2, 1)
    fc.finish(slice(2 * quarter, 3 * quarter))
    fd.finish(slice(3 * quarter, block))

    for group in range(4):
        group_copy(group // 2, group % 2).wait_send()
    for copy in started:
        copy.wait_send()


def fused_body(tokens, quant_weight, block_scales, key_grad):
    row_count, model = tokens.shape
    shard_rows, width = quant_weight.shape
    block = model // (lax.axis_size("rep") * lax.axis_size("fsdp"))
    bf16, f32 = jnp.bfloat16, jnp.float32
    vmem = pl.BlockSpec(memory_space=pltpu.VMEM)
    hbm = pl.BlockSpec(memory_space=pltpu.HBM)
    flows = [
        pltpu.VMEM((2,) * (4 - level) + (block // 4, width), bf16)
        for level in range(5)
        for _ in range(4)
    ]
    results = pl.pallas_call(
        fused_kernel,
        out_shape=[
            pltpu.VMEM((row_count, width), bf16),
            pltpu.VMEM((row_count, model), bf16),
            pltpu.VMEM((block, width), bf16),
        ],
        in_specs=[hbm, hbm, vmem, hbm],
        out_specs=[vmem] * 3,
        scratch_shapes=[
            pltpu.VMEM((row_count, model), bf16),
            pltpu.VMEM((shard_rows, width), bf16),
            pltpu.VMEM((row_count, width), bf16),
            pltpu.VMEM((row_count, width), bf16),
            pltpu.VMEM((4, 8, shard_rows // 8, width), bf16),
            pltpu.VMEM((2, 2, row_count, 4 * block), bf16),
            pltpu.VMEM((2, row_count, width), bf16),
            pltpu.VMEM((row_count, width), f32),
            pltpu.VMEM((2, row_count, HEAD_DIM), f32),
            pltpu.VMEM((2, row_count, HEAD_DIM), f32),
            *flows,
            pltpu.SemaphoreType.DMA((3,)),
            pltpu.SemaphoreType.DMA((8,)),
            pltpu.SemaphoreType.DMA((2,)),
            pltpu.SemaphoreType.DMA((17,)),
            pltpu.SemaphoreType.DMA((17,)),
            pltpu.SemaphoreType.DMA((32,)),
            pltpu.SemaphoreType.DMA((32,)),
        ],
        compiler_params=pltpu.CompilerParams(
            collective_id=0, has_side_effects=True, vmem_limit_bytes=56 * 1024 * 1024
        ),
    )(tokens, quant_weight, block_scales, key_grad)
    return pl.pallas_call(
        place_kernel,
        out_shape=[jax.ShapeDtypeStruct(value.shape, value.dtype) for value in results],
        in_specs=[vmem] * 3,
        out_specs=[hbm] * 3,
        scratch_shapes=[pltpu.SemaphoreType.DMA((3,))],
        compiler_params=pltpu.CompilerParams(vmem_limit_bytes=4 * 1024 * 1024),
    )(*results)


def place_kernel(rot_in, tg_in, wg_in, rot_out, tg_out, wg_out, sems):
    pairs = ((tg_in, tg_out), (rot_in, rot_out), (wg_in, wg_out))
    copies = [
        pltpu.make_async_copy(source, target, sems.at[i])
        for i, (source, target) in enumerate(pairs)
    ]
    for copy in copies:
        copy.start()
    for copy in copies:
        copy.wait()


def solution(mesh):
    paired = mesh.shape["rep"] == 8 and mesh.shape["fsdp"] == 4
    return jax.shard_map(
        fused_body if paired else body,
        mesh=mesh,
        in_specs=(P(("rep", "fsdp"), None), P("fsdp", None), P("fsdp"), P(("rep", "fsdp"), None)),
        out_specs=(P(("rep", "fsdp"), None), P(("rep", "fsdp"), None), P(("rep", "fsdp"), None)),
        check_vma=False,
    )
```
